32 devices in a mesh: ctx: 8 (over z, core), grp: 4 (over y, x).
Axes of the slice: x: 2, y: 2, z: 4, core: 2. Of those that a mesh axis runs over, the one named last changes fastest.
Arguments:
- queries: bfloat16 [1, 4096, 4096], P(None, ('ctx', 'grp')), may hold values from -200 to 200
- keyvals: bfloat16 [2, 1, 4096, 512], P(None, None, ('ctx', 'grp')), may hold values from -8 to 8
- seg_len: int32 [1, 16], replicated, may hold values from 128 to 384, as said below
- seg_task: int32 [1, 16], replicated, may hold values from 0 to 23
- task_slot: int32 [24], replicated, may hold values from 0 to 23, each once
- prefix_bank: bfloat16 [2, 24, 16, 512], P(None, 'grp'), may hold values from -9 to 9
Outputs:
- attended: bfloat16 [1, 4096, 4096], P(None, ('ctx', 'grp'))
The draws below stay inside these ranges and needn't reach their ends.
Inputs may be any that keep to these rules, and one draw needn't show every extreme that they name: `seg_len`: the 16 lengths sum to 4096, and at least one equals 384. `task_slot`: A permutation; bank row r is held by index r // 6 of grp.
All inputs are finite; a program needn't handle non-finite values.
Results may differ from the reference program's by a relative error of at most 0.004.
Values may be sent and summed in bfloat16 or wider, within the bound.
No kernel may reach another device: no remote copies, remote signals or barrier semaphores. Data moves between devices by JAX's collectives and lax.ppermute only.
A program may use at most 64 MiB of HBM per device.

```python
import math
import jax
import jax.numpy as jnp
from jax import lax

H = 32
KVH = 4
HD = 128
T_DEV = 128
PREFIX = 16
HOPS = 3
ROWS = 1
ROW_LEN = 4096
MOST = 384
SEGS = 16
TASKS = 24


def joint_draw(key):
    base = jax.random.fold_in(key, 11)
    key_q, key_k, key_v = jax.random.split(base, 3)
    groups = H // KVH
    keys_all = jnp.clip(jax.random.normal(key_k, (ROWS, ROW_LEN, KVH, HD), jnp.float32), -6.0, 6.0)
    values_all = jnp.clip(jax.random.normal(key_v, (ROWS, ROW_LEN, KVH, HD), jnp.float32), -6.0, 6.0)
    queries_all = jnp.clip(jax.random.normal(key_q, (ROWS, ROW_LEN, KVH, groups, HD), jnp.float32), -6.0, 6.0)
    return (queries_all, keys_all, values_all)


def draw_queries(key, part):
    queries_all, keys_all, values_all = joint_draw(key)
    return queries_all.reshape(ROWS, ROW_LEN, H * HD).astype(jnp.bfloat16)


def draw_keyvals(key, part):
    queries_all, keys_all, values_all = joint_draw(key)
    stacked = jnp.stack([keys_all.reshape(ROWS, ROW_LEN, KVH * HD), values_all.reshape(ROWS, ROW_LEN, KVH * HD)])
    return stacked.astype(jnp.bfloat16)


def draw_seg_len(key, part):
    key_split, key_order = jax.random.split(jax.random.fold_in(key, 23))
    pair_count = (ROW_LEN // T_DEV - HOPS) // (HOPS + 1)
    moved = jax.random.randint(key_split, (ROWS, pair_count), 0, (HOPS - 1) * T_DEV + 1)
    first_part = T_DEV + moved
    second_part = HOPS * T_DEV - moved
    paired = jnp.stack([first_part, second_part], axis=2).reshape(ROWS, 2 * pair_count)
    listed = jnp.concatenate([paired, jnp.full((ROWS, 1), T_DEV, jnp.int32), jnp.full((ROWS, 1), MOST, jnp.int32)], axis=1).astype(jnp.int32)
    orders = jax.vmap(lambda sub_key: jax.random.permutation(sub_key, SEGS))(jax.random.split(key_order, ROWS))
    return jnp.take_along_axis(listed, orders.astype(jnp.int32), axis=1).astype(jnp.int32)


def with_ends(entries, own_key, low, top_value):
    spot = [jax.random.randint(jax.random.fold_in(own_key, axis), (), 0, length) for axis, length in enumerate(entries.shape)]
    main_axis = entries.shape.index(max(entries.shape))
    neighbour = spot[:main_axis] + [(spot[main_axis] + 1) % entries.shape[main_axis]] + spot[main_axis + 1:]
    return entries.at[tuple(spot)].set(low).at[tuple(neighbour)].set(top_value)


def levels(stream_key, extent, pieces, low, largest):
    loudness = 1.0
    for axis_at, shards_of in pieces:
        heights = jax.random.uniform(jax.random.fold_in(jax.random.fold_in(stream_key, 6), axis_at), (shards_of,), jnp.float32, low / len(pieces), largest / len(pieces))
        loudness = loudness * jnp.repeat(jnp.exp(heights), extent[axis_at] // shards_of).reshape((-1,) + (1,) * (len(extent) - 1 - axis_at))
    return loudness


def normal_values(own_key, shape, scale, bound, shards=(), kind=jnp.bfloat16):
    loudness = levels(own_key, shape, shards, -0.22, 0.18) if shards else 1.0
    array = jax.random.normal(own_key, shape, jnp.float32) * scale * loudness
    return jnp.minimum(jnp.maximum(array, -bound), bound).astype(kind)


def setup_inputs(seed: int = 0) -> dict:
    streams_of = jax.random.split(jax.random.key(seed), 7)
    return {
        "queries": draw_queries(jax.random.fold_in(streams_of[6], 71), 0),
        "keyvals": draw_keyvals(jax.random.fold_in(streams_of[6], 71), 0),
        "seg_len": draw_seg_len(jax.random.fold_in(streams_of[6], 71), 0),
        "seg_task": with_ends(jax.random.randint(streams_of[3], (ROWS, SEGS), 0, TASKS), jax.random.fold_in(streams_of[3], 1), 0, TASKS - 1).astype(jnp.int32),
        "task_slot": jax.random.permutation(streams_of[4], TASKS).astype(jnp.int32),
        "prefix_bank": normal_values(streams_of[5], (2, TASKS, PREFIX, KVH * HD), 1.5, 9.0, ((1, 4),)),
    }


def segment_index(starts, positions):
    return lax.optimization_barrier(jnp.sum((starts[None, :] <= positions[:, None]).astype(jnp.int32), axis=1)) - 1

def reference(queries, keyvals, seg_len, seg_task, task_slot, prefix_bank):
    groups = H // KVH
    score_scale = 1.0 / math.sqrt(HD)
    window_len = MOST + T_DEV

    def one_row(row_index):
        row_q = queries[row_index]
        row_kv = keyvals[:, row_index]
        lengths = seg_len[row_index]
        row_tasks = seg_task[row_index]
        starts = jnp.cumsum(lengths) - lengths
        padded = jnp.concatenate([jnp.zeros((2, MOST, KVH * HD), keyvals.dtype), row_kv], axis=1)

        def one_block(block_index):
            first = block_index * T_DEV
            block_q = lax.dynamic_slice_in_dim(row_q, first, T_DEV, 0).reshape(T_DEV, KVH, groups, HD).astype(jnp.float32)
            window = lax.dynamic_slice_in_dim(padded, first, window_len, 1).reshape(2, window_len, KVH, HD).astype(jnp.float32)
            query_pos = first + jnp.arange(T_DEV, dtype=jnp.int32)
            key_pos = first - MOST + jnp.arange(window_len, dtype=jnp.int32)
            query_seg = segment_index(starts, query_pos)
            key_seg = segment_index(starts, key_pos)
            allowed = (key_seg[None, :] == query_seg[:, None]) & (key_pos[None, :] <= query_pos[:, None])
            query_task = row_tasks[query_seg]
            bank_row = task_slot[query_task]
            prefix = prefix_bank[:, bank_row].reshape(2, T_DEV, PREFIX, KVH, HD).astype(jnp.float32)
            local_scores = jnp.einsum('tkgd,skd->kgts', block_q, window[0]) * score_scale
            prefix_scores = jnp.einsum('tkgd,tpkd->kgtp', block_q, prefix[0]) * score_scale
            scores = jnp.concatenate([local_scores, prefix_scores], axis=-1)
            mask_full = jnp.concatenate([jnp.broadcast_to(allowed, (KVH, groups, T_DEV, window_len)), jnp.ones((KVH, groups, T_DEV, PREFIX), dtype=bool)], axis=-1)
            top_score = lax.optimization_barrier(jnp.max(jnp.where(mask_full, scores, -jnp.inf), axis=-1, keepdims=True))
            weights = jnp.where(mask_full, jnp.exp(scores - top_score), 0.0)
            total = lax.optimization_barrier(jnp.sum(weights, axis=-1))
            rounded = lax.optimization_barrier(weights.astype(jnp.bfloat16)).astype(jnp.float32)
            mixed = jnp.einsum('kgts,skd->kgtd', rounded[..., :window_len], window[1])
            mixed = mixed + jnp.einsum('kgtp,tpkd->kgtd', rounded[..., window_len:], prefix[1])
            result = mixed / total[..., None]
            return result.transpose(2, 0, 1, 3).reshape(T_DEV, H * HD).astype(jnp.bfloat16)
        blocks = lax.map(one_block, jnp.arange(ROW_LEN // T_DEV, dtype=jnp.int32))
        return blocks.reshape(ROW_LEN, H * HD)
    return lax.map(one_row, jnp.arange(ROWS, dtype=jnp.int32))
```

```python
import functools
import math

import jax
import jax.numpy as jnp
from jax import lax
from jax.experimental import pallas as pl
from jax.experimental.pallas import tpu as pltpu
from jax.sharding import PartitionSpec as P

HD = 128
HOPS = 3
FAR = -1e30
AXES = ("ctx", "grp")
VMEM = pl.BlockSpec(memory_space=pltpu.VMEM)
SMEM = pl.BlockSpec(memory_space=pltpu.SMEM)
PARAMS = pltpu.CompilerParams(vmem_limit_bytes=40 * 2**20)


def shift_route(count, distance):
    return [(i, (i + distance) % count) for i in range(count)]


def flip_route(ctx_count, grp_count, flip):
    count = ctx_count * grp_count
    return [
        (i, (i + ((i % grp_count ^ flip) - i % grp_count) % grp_count) % count)
        for i in range(count)
    ]


def compose_route(wanted, first):
    holder = dict(first)
    return [(holder[s], d) for s, d in wanted]


def shard_segments(len_ref, firsts, shard_len):
    def step(s, carry):
        start, found = carry
        out = []
        for first, (seg_a, start_a, seg_b, start_b) in zip(firsts, found):
            in_a = start <= first
            in_b = start <= first + (shard_len - 1)
            out.append(
                (
                    jnp.where(in_a, s, seg_a),
                    jnp.where(in_a, start, start_a),
                    jnp.where(in_b, s, seg_b),
                    jnp.where(in_b, start, start_b),
                )
            )
        return start + len_ref[0, s], out

    zero = jnp.int32(0)
    _, found = lax.fori_loop(
        0, len_ref.shape[1], step, (zero, [(zero, zero, zero, zero)] * len(firsts))
    )
    return found


def bank_rows(task_ref, slot_ref, found):
    seg_a, _, seg_b, _ = found
    return slot_ref[task_ref[0, seg_a]], slot_ref[task_ref[0, seg_b]]


def pick_kernel(shard_len, offsets, len_ref, task_ref, slot_ref, bank_ref, *out_refs):
    grp_count = lax.axis_size("grp")
    me = lax.axis_index("grp")
    row_base = lax.axis_index("ctx") * grp_count
    held = bank_ref.shape[1]
    firsts = [(row_base + (me ^ k)) * shard_len for k in offsets]
    for out_ref, found in zip(out_refs, shard_segments(len_ref, firsts, shard_len)):
        for slot, row in enumerate(bank_rows(task_ref, slot_ref, found)):
            local = jnp.clip(row - me * held, 0, held - 1)
            for kind in range(2):
                out_ref[slot, kind] = bank_ref[kind, local]


def attend(q_ref, head, groups, keys, values, masks):
    t = q_ref.shape[1]
    cols = [q_ref[0, :, pl.ds((head * groups + g) * HD, HD)] for g in range(groups)]
    eye = (
        lax.broadcasted_iota(jnp.int32, (t, t), 0) == lax.broadcasted_iota(jnp.int32, (t, t), 1)
    ).astype(jnp.float32).astype(jnp.bfloat16)
    q = jnp.concatenate(cols, axis=0)
    q = jnp.concatenate([q, jnp.concatenate([eye] * groups, axis=0)], axis=1)
    k = jnp.concatenate([keys, masks], axis=1)
    s = lax.dot_general(q, k, (((1,), (1,)), ((), ())), preferred_element_type=jnp.float32)
    top = jnp.max(s, axis=1, keepdims=True)
    w = jnp.exp2((s - top) * (math.log2(math.e) / math.sqrt(HD))).astype(jnp.bfloat16)
    v = jnp.concatenate([values, jnp.ones(values.shape, jnp.bfloat16)], axis=1)
    o = jnp.dot(w, v, preferred_element_type=jnp.float32)
    return top, o[:, :HD], o[:, HD:]


def block_mask(first, hop, start_a, start_b, shard_len):
    shape = (shard_len, shard_len)
    key = lax.broadcasted_iota(jnp.int32, shape, 0) - hop * shard_len
    query = lax.broadcasted_iota(jnp.int32, shape, 1)
    from_b = start_b - first
    start = jnp.where(query >= from_b, from_b, start_a - first)
    allowed = (key >= start) & (key <= query)
    return jnp.where(allowed, 0.0, FAR).astype(jnp.bfloat16)


def hop_of(kind, grp_count):
    me = lax.axis_index("grp")
    if kind[0] == "shift":
        return kind[1]
    return (me - (me ^ kind[1])) & (grp_count - 1)


def early_kernel(kinds, groups, len_ref, q_ref, *refs):
    kv_refs = refs[: len(kinds)]
    acc_ref, sum_ref, top_ref = refs[len(kinds) :]
    t = q_ref.shape[1]
    kv_heads = kv_refs[0].shape[-1] // HD
    grp_count = lax.axis_size("grp")
    first = (lax.axis_index("ctx") * grp_count + lax.axis_index("grp")) * t
    (_, start_a, _, start_b), = shard_segments(len_ref, [first], t)
    masks = jnp.concatenate(
        [block_mask(first, hop_of(kind, grp_count), start_a, start_b, t) for kind in kinds], axis=0
    )
    for head in range(kv_heads):
        lanes = pl.ds(head * HD, HD)
        keys = jnp.concatenate([r[0, 0, :, lanes] for r in kv_refs], axis=0)
        values = jnp.concatenate([r[1, 0, :, lanes] for r in kv_refs], axis=0)
        top, acc, total = attend(q_ref, head, groups, keys, values, masks)
        for g in range(groups):
            rows = slice(g * t, (g + 1) * t)
            out = pl.ds((head * groups + g) * HD, HD)
            acc_ref[:, out] = acc[rows]
            sum_ref[:, out] = total[rows]
            top_ref[:, out] = jnp.broadcast_to(top[rows], (t, HD))


def late_kernel(kind, groups, len_ref, task_ref, slot_ref, q_ref, k_ref, v_ref, *refs):
    prefix_refs = refs[:-4]
    acc_ref, sum_ref, top_ref, out_ref = refs[-4:]
    t = q_ref.shape[1]
    kv_heads = k_ref.shape[-1] // HD
    grp_count = lax.axis_size("grp")
    me = lax.axis_index("grp")
    first = (lax.axis_index("ctx") * grp_count + me) * t
    found, = shard_segments(len_ref, [first], t)
    _, start_a, _, start_b = found
    prefix_len, width = prefix_refs[0].shape[2:]
    held = slot_ref.shape[0] // grp_count
    picked = []
    for slot, row in enumerate(bank_rows(task_ref, slot_ref, found)):
        pair = []
        for part in range(2):
            if len(prefix_refs) == 1:
                pair.append(prefix_refs[0][slot, part])
                continue
            place = (row // held) ^ me
            value = prefix_refs[0][slot, part]
            for k in range(1, len(prefix_refs)):
                value = jnp.where(place == k, prefix_refs[k][slot, part], value)
            pair.append(value)
        picked.append(pair)
    shape = (prefix_len, t)
    is_b = lax.broadcasted_iota(jnp.int32, shape, 1) >= start_b - first
    mask_a = jnp.where(is_b, FAR, 0.0).astype(jnp.bfloat16)
    mask_b = jnp.where(is_b, 0.0, FAR).astype(jnp.bfloat16)
    masks = jnp.concatenate(
        [block_mask(first, hop_of(kind, grp_count), start_a, start_b, t), mask_a, mask_b], axis=0
    )
    scale = math.log2(math.e) / math.sqrt(HD)
    for head in range(kv_heads):
        lanes = pl.ds(head * HD, HD)
        cut = slice(head * HD, (head + 1) * HD)
        keys = jnp.concatenate([k_ref[0, 0, :, lanes]] + [p[0][:, cut] for p in picked], axis=0)
        values = jnp.concatenate([v_ref[0, 0, :, lanes]] + [p[1][:, cut] for p in picked], axis=0)
        top, acc, total = attend(q_ref, head, groups, keys, values, masks)
        for g in range(groups):
            rows = slice(g * t, (g + 1) * t)
            at = pl.ds((head * groups + g) * HD, HD)
            old = top_ref[:, at]
            new = jnp.broadcast_to(top[rows], (t, HD))
            best = jnp.maximum(old, new)
            keep = jnp.exp2((old - best) * scale)
            take = jnp.exp2((new - best) * scale)
            mixed = acc_ref[:, at] * keep + acc[rows] * take
            out_ref[0, :, at] = (mixed / (sum_ref[:, at] * keep + total[rows] * take)).astype(
                out_ref.dtype
            )


def on_device(queries, keyvals, seg_len, seg_task, task_slot, prefix_bank):
    ctx_count, grp_count = (lax.axis_size(a) for a in AXES)
    count = ctx_count * grp_count
    t = queries.shape[1]
    groups = queries.shape[2] // keyvals.shape[3]
    prefix_shape = (2, 2) + prefix_bank.shape[2:]
    plane = grp_count == HOPS + 1

    if plane:
        kinds = [("flip", k) for k in (1, 2, 3)]
        near, side, far = (flip_route(ctx_count, grp_count, k) for k in (1, 2, 3))
        got_near = lax.ppermute(keyvals, AXES, near)
        got_side = lax.ppermute(keyvals, AXES, side)
        far_keys = lax.ppermute(got_side[0:1], AXES, compose_route(far, side))
        far_values = lax.ppermute(got_near[1:2], AXES, compose_route(far, near))
        offsets = range(grp_count)
        prefix = pl.pallas_call(
            functools.partial(pick_kernel, t, offsets),
            out_shape=[jax.ShapeDtypeStruct(prefix_shape, prefix_bank.dtype)] * grp_count,
            in_specs=[SMEM] * 3 + [VMEM],
            out_specs=[VMEM] * grp_count,
            compiler_params=PARAMS,
            name="pick_prefix",
        )(seg_len, seg_task, task_slot, prefix_bank)
        prefix = [prefix[0]] + [
            lax.ppermute(prefix[k], "grp", [(i, i ^ k) for i in range(grp_count)])
            for k in offsets[1:]
        ]
    else:
        kinds = [("shift", d) for d in range(1, HOPS + 1)]
        got_near, got_side, got_far = (
            lax.ppermute(keyvals, AXES, shift_route(count, d)) for d in range(1, HOPS + 1)
        )
        far_keys, far_values = got_far[0:1], got_far[1:2]
        prefix = [fetch_prefix(seg_len, seg_task, task_slot, prefix_bank, t)]

    wide = jax.ShapeDtypeStruct(queries.shape[1:], jnp.float32)
    early = [("shift", 0)] + kinds[:2]
    cost = 2 * 2 * queries.size * t
    state = pl.pallas_call(
        functools.partial(early_kernel, early, groups),
        out_shape=[wide] * 3,
        in_specs=[SMEM] + [VMEM] * 4,
        out_specs=[VMEM] * 3,
        compiler_params=PARAMS,
        cost_estimate=pl.CostEstimate(
            flops=3 * cost, bytes_accessed=2 * queries.size, transcendentals=3 * queries.size
        ),
        name="attend_near",
    )(seg_len, queries, keyvals, got_near, got_side)
    return pl.pallas_call(
        functools.partial(late_kernel, kinds[2], groups),
        out_shape=jax.ShapeDtypeStruct(queries.shape, queries.dtype),
        in_specs=[SMEM] * 3 + [VMEM] * (6 + len(prefix)),
        out_specs=VMEM,
        compiler_params=PARAMS,
        cost_estimate=pl.CostEstimate(
            flops=cost, bytes_accessed=4 * queries.size, transcendentals=queries.size
        ),
        name="attend_far",
    )(seg_len, seg_task, task_slot, queries, far_keys, far_values, *prefix, *state)


def fetch_prefix(seg_len, seg_task, task_slot, prefix_bank, t):
    grp_count = lax.axis_size("grp")
    me = lax.axis_index("grp")
    held = prefix_bank.shape[1]
    starts = jnp.cumsum(seg_len[0]) - seg_len[0]
    shards = lax.axis_index("ctx") * grp_count + jnp.arange(grp_count, dtype=jnp.int32)
    ends = shards[:, None] * t + jnp.array([0, t - 1], jnp.int32)
    segs = jnp.sum((starts[None, None, :] <= ends[:, :, None]).astype(jnp.int32), axis=2) - 1
    rows = task_slot[seg_task[0][segs]]
    local = jnp.clip(rows - me * held, 0, held - 1)
    pieces = jnp.swapaxes(prefix_bank, 0, 1)[local]
    got = lax.all_to_all(pieces, "grp", split_axis=0, concat_axis=0, tiled=True)
    owner = rows[me] // held
    return jnp.stack([got[owner[s], s] for s in range(2)])


def solution(mesh):
    in_specs = (
        P(None, AXES, None),
        P(None, None, AXES, None),
        P(),
        P(),
        P(),
        P(None, "grp", None, None),
    )
    return jax.shard_map(
        on_device, mesh=mesh, in_specs=in_specs, out_specs=P(None, AXES, None), check_vma=False
    )
```

```python
import functools
import math

import jax
import jax.numpy as jnp
from jax import lax
from jax.experimental import pallas as pl
from jax.experimental.pallas import tpu as pltpu
from jax.sharding import PartitionSpec as P

HD = 128
HOPS = 3
FAR = -1e30
AXES = ("ctx", "grp")
VMEM = pl.BlockSpec(memory_space=pltpu.VMEM)
HBM = pl.BlockSpec(memory_space=pltpu.HBM)
SCALE = math.log2(math.e) / math.sqrt(HD)
PARAMS = pltpu.CompilerParams(vmem_limit_bytes=40 * 2**20)


def shift_route(count, distance):
    return [(i, (i + distance) % count) for i in range(count)]


def flip_route(ctx_count, grp_count, flip):
    count = ctx_count * grp_count
    return [
        (i, (i + ((i % grp_count ^ flip) - i % grp_count) % grp_count) % count)
        for i in range(count)
    ]


def compose_route(wanted, first):
    holder = dict(first)
    return [(holder[s], d) for s, d in wanted]


def shard_segments(len_ref, firsts, shard_len):
    def step(s, carry):
        start, found = carry
        out = []
        for first, (seg_a, start_a, seg_b, start_b) in zip(firsts, found):
            in_a = start <= first
            in_b = start <= first + (shard_len - 1)
            out.append(
                (
                    jnp.where(in_a, s, seg_a),
                    jnp.where(in_a, start, start_a),
                    jnp.where(in_b, s, seg_b),
                    jnp.where(in_b, start, start_b),
                )
            )
        return start + len_ref[0, s], out

    zero = jnp.int32(0)
    _, found = lax.fori_loop(
        0, len_ref.shape[1], step, (zero, [(zero, zero, zero, zero)] * len(firsts))
    )
    return found


def bank_rows(task_ref, slot_ref, found):
    seg_a, _, seg_b, _ = found
    return slot_ref[task_ref[0, seg_a]], slot_ref[task_ref[0, seg_b]]


def block_mask(first, hop, start_a, start_b, t):
    key = lax.broadcasted_iota(jnp.int32, (t, t), 0) - hop * t
    query = lax.broadcasted_iota(jnp.int32, (t, t), 1)
    from_b = start_b - first
    start = jnp.where(query >= from_b, from_b, start_a - first)
    return jnp.where((key >= start) & (key <= query), 0.0, FAR).astype(jnp.bfloat16)


def hop_of(kind, grp_count):
    me = lax.axis_index("grp")
    if kind[0] == "shift":
        return kind[1]
    return (me - (me ^ kind[1])) & (grp_count - 1)


def plan_kernel(t, kinds, sends, len_hbm, task_hbm, slot_hbm, bank_hbm, *refs):
    mask_ref, place_ref, out_refs = refs[0], refs[1], refs[2 : 2 + len(sends)]
    len_ref, task_ref, slot_ref, bank_ref, sems = refs[2 + len(sends) :]
    pairs = ((len_hbm, len_ref), (task_hbm, task_ref), (slot_hbm, slot_ref), (bank_hbm, bank_ref))
    copies = [pltpu.make_async_copy(a, b, sems.at[i]) for i, (a, b) in enumerate(pairs)]
    for copy in copies:
        copy.start()
    for copy in copies[:3]:
        copy.wait()
    grp_count = lax.axis_size("grp")
    me = lax.axis_index("grp")
    row_base = lax.axis_index("ctx") * grp_count
    held = bank_ref.shape[1]
    shards = [row_base + me] + [row_base + (me ^ k) for k in sends[1:]]
    found = shard_segments(len_ref, [s * t for s in shards], t)
    first = shards[0] * t
    _, start_a, _, start_b = found[0]
    size = bank_ref.shape[2]
    is_b = lax.broadcasted_iota(jnp.int32, (size, t), 1) >= start_b - first
    blocks = [block_mask(first, hop_of(k, grp_count), start_a, start_b, t) for k in kinds]
    blocks[-1:-1] = [jnp.where(is_b, a, b).astype(jnp.bfloat16) for a, b in ((FAR, 0.0), (0.0, FAR))]
    mask_ref[...] = jnp.concatenate(blocks, axis=0)
    rows = [bank_rows(task_ref, slot_ref, f) for f in found]
    for slot, row in enumerate(rows[0]):
        place_ref[slot] = jnp.full(place_ref.shape[1:], (row // held) ^ me, jnp.int32)
    copies[3].wait()
    for out_ref, pair in zip(out_refs, rows):
        for slot, row in enumerate(pair):
            local = jnp.clip(row - me * held, 0, held - 1)
            for part in range(2):
                out_ref[slot, part] = bank_ref[part, local]


def eye(t):
    a, b = (lax.broadcasted_iota(jnp.int32, (t, t), i) for i in range(2))
    return (a == b).astype(jnp.float32).astype(jnp.bfloat16)


def staged(count, score, weigh, mix):
    scores, weights = {}, {}
    for i in range(count + 2):
        if i < count:
            scores[i] = score(i)
        if 0 <= i - 1 < count:
            weights[i - 1] = weigh(i - 1, scores.pop(i - 1))
        if 0 <= i - 2 < count:
            mix(i - 2, weights.pop(i - 2))


def score(keys, masks, q, ones):
    return jnp.dot(
        jnp.concatenate([keys, masks], axis=1),
        jnp.concatenate([q, ones], axis=0),
        preferred_element_type=jnp.float32,
    )


def mix(values, weights):
    v = jnp.concatenate([values.T, jnp.ones((16, values.shape[0]), jnp.bfloat16)], axis=0)
    return jnp.dot(v, weights, preferred_element_type=jnp.float32)


def pick_prefix(place_ref, prefix_refs):
    picked = [[], []]
    for part in range(2):
        for slot in range(2):
            value = prefix_refs[0][slot, part]
            for k in range(1, len(prefix_refs)):
                here = jnp.broadcast_to(place_ref[slot][:1, :1] == k, value.shape)
                value = jnp.where(here, prefix_refs[k][slot, part], value)
            picked[part].append(value)
    return picked


def near_kernel(groups, sends, mask_ref, place_ref, q_hbm, own_hbm, *refs):
    prefix_refs, kv_refs = refs[:sends], refs[sends:-8]
    qt_ref, acc_ref, sum_ref, top_ref, q_ref, own_ref, q_sems, own_sem = refs[-8:]
    own_copy = pltpu.make_async_copy(own_hbm, own_ref, own_sem)
    own_copy.start()
    q_copies = []
    for j in range(acc_ref.shape[0]):
        cols = pl.ds(j * groups * HD, groups * HD)
        q_copies.append(
            pltpu.make_async_copy(q_hbm.at[:, :, cols], q_ref.at[:, :, cols], q_sems.at[j])
        )
        q_copies[-1].start()
    kv_refs = (own_ref,) + tuple(kv_refs)
    t = q_ref.shape[1]
    picked = pick_prefix(place_ref, prefix_refs)
    masks = mask_ref[: len(kv_refs) * t + 2 * picked[0][0].shape[0], :]
    ones = jnp.concatenate([eye(t)] * groups, axis=1)
    own_copy.wait()

    def lanes(j):
        return slice(j * HD, (j + 1) * HD)

    def rows(part, j):
        return jnp.concatenate(
            [r[part, 0, :, lanes(j)] for r in kv_refs] + [p[:, lanes(j)] for p in picked[part]],
            axis=0,
        )

    def scored(j):
        q_copies[j].wait()
        q = jnp.concatenate([q_ref[0, :, lanes(j * groups + g)].T for g in range(groups)], axis=1)
        qt_ref[j] = q
        return score(rows(0, j), masks, q, ones)

    def weighed(j, s):
        top = jnp.max(s, axis=0, keepdims=True) * SCALE
        top_ref[j : j + 1, :] = top
        return jnp.exp2(s * SCALE - top).astype(jnp.bfloat16)

    def mixed(j, w):
        o = mix(rows(1, j), w)
        acc_ref[j] = o[:HD]
        sum_ref[j : j + 1, :] = o[HD : HD + 1]

    staged(acc_ref.shape[0], scored, weighed, mixed)


def far_kernel(groups, mask_ref, k_ref, v_ref, *refs):
    qt_ref, acc_ref, sum_ref, top_ref, out_hbm, out_ref, sems = refs
    t = k_ref.shape[2]
    masks = mask_ref[mask_ref.shape[0] - t :, :]
    ones = jnp.concatenate([eye(t)] * groups, axis=1)
    copies = []

    def lanes(j):
        return slice(j * HD, (j + 1) * HD)

    def scored(j):
        return score(k_ref[0, 0, :, lanes(j)], masks, qt_ref[j], ones)

    def weighed(j, s):
        old = top_ref[j : j + 1, :]
        top = jnp.maximum(jnp.max(s, axis=0, keepdims=True) * SCALE, old)
        return jnp.exp2(s * SCALE - top).astype(jnp.bfloat16), jnp.exp2(old - top)

    def mixed(j, pair):
        w, keep = pair
        o = mix(v_ref[0, 0, :, lanes(j)], w)
        total = sum_ref[j : j + 1, :] * keep + o[HD : HD + 1]
        part = 1.0 / total
        done = acc_ref[j] * (keep * part) + o[:HD] * part
        for g in range(groups):
            out_ref[0, :, lanes(j * groups + g)] = (
                done[:, g * t : (g + 1) * t].T.astype(out_ref.dtype)
            )
        cols = pl.ds(j * groups * HD, groups * HD)
        copies.append(
            pltpu.make_async_copy(out_ref.at[:, :, cols], out_hbm.at[:, :, cols], sems.at[j])
        )
        copies[-1].start()

    staged(acc_ref.shape[0], scored, weighed, mixed)
    for copy in copies:
        copy.wait()


def on_device(queries, keyvals, seg_len, seg_task, task_slot, prefix_bank):
    ctx_count, grp_count = (lax.axis_size(a) for a in AXES)
    t = queries.shape[1]
    kv_heads = keyvals.shape[3] // HD
    groups = queries.shape[2] // keyvals.shape[3]
    plane = grp_count == HOPS + 1
    prefix_shape = (2, 2) + prefix_bank.shape[2:]
    if plane:
        kinds = [("shift", 0)] + [("flip", k) for k in range(1, HOPS + 1)]
        sends = range(grp_count)
        near, side, far = (flip_route(ctx_count, grp_count, k) for k in range(1, HOPS + 1))
    else:
        kinds = [("shift", d) for d in range(HOPS + 1)]
        sends = range(0)
        near, side, far = (shift_route(ctx_count * grp_count, d) for d in range(1, HOPS + 1))

    got_near = lax.ppermute(keyvals, AXES, near)
    got_side = lax.ppermute(keyvals, AXES, side)

    def struct(shape, dtype):
        return jax.ShapeDtypeStruct(shape, dtype)

    def in_hbm(array):
        return pltpu.with_memory_space_constraint(array, pltpu.HBM)

    masks, place, *rows = pl.pallas_call(
        functools.partial(plan_kernel, t, kinds, sends),
        out_shape=[
            struct((len(kinds) * t + 2 * prefix_shape[2], t), jnp.bfloat16),
            struct((2, 8, 128), jnp.int32),
        ]
        + [struct(prefix_shape, prefix_bank.dtype)] * len(sends),
        in_specs=[HBM] * 4,
        out_specs=[VMEM] * (2 + len(sends)),
        scratch_shapes=[pltpu.SMEM(a.shape, a.dtype) for a in (seg_len, seg_task, task_slot)]
        + [pltpu.VMEM(prefix_bank.shape, prefix_bank.dtype), pltpu.SemaphoreType.DMA((4,))],
        compiler_params=PARAMS,
        name="plan",
    )(*(in_hbm(a) for a in (seg_len, seg_task, task_slot, prefix_bank)))
    if plane:
        prefix = [rows[0]] + [
            lax.ppermute(rows[k], "grp", [(i, i ^ k) for i in range(grp_count)]) for k in sends[1:]
        ]
        far_keys = lax.ppermute(got_side[0:1], AXES, compose_route(far, side))
        far_values = lax.ppermute(got_near[1:2], AXES, compose_route(far, near))
    else:
        prefix = [fetch_prefix(seg_len, seg_task, task_slot, prefix_bank, t)]
        got_far = lax.ppermute(keyvals, AXES, far)
        far_keys, far_values = got_far[0:1], got_far[1:2]

    wide = struct((kv_heads, HD, groups * t), jnp.float32)
    flat = struct((kv_heads, groups * t), jnp.float32)
    cost = 4 * queries.size * t
    state = pl.pallas_call(
        functools.partial(near_kernel, groups, len(prefix)),
        out_shape=[struct(wide.shape, queries.dtype), wide, flat, flat],
        in_specs=[VMEM, VMEM, HBM, HBM] + [VMEM] * (len(prefix) + 2),
        out_specs=[VMEM] * 4,
        scratch_shapes=[
            pltpu.VMEM(queries.shape, queries.dtype),
            pltpu.VMEM(keyvals.shape, keyvals.dtype),
            pltpu.SemaphoreType.DMA((kv_heads,)),
            pltpu.SemaphoreType.DMA,
        ],
        compiler_params=PARAMS,
        cost_estimate=pl.CostEstimate(
            flops=3 * cost, bytes_accessed=2 * queries.size, transcendentals=3 * queries.size
        ),
        name="attend_near",
    )(masks, place, in_hbm(queries), in_hbm(keyvals), *prefix, got_near, got_side)
    return pl.pallas_call(
        functools.partial(far_kernel, groups),
        out_shape=struct(queries.shape, queries.dtype),
        in_specs=[VMEM] * 7,
        out_specs=HBM,
        scratch_shapes=[
            pltpu.VMEM(queries.shape, queries.dtype),
            pltpu.SemaphoreType.DMA((kv_heads,)),
        ],
        compiler_params=PARAMS,
        cost_estimate=pl.CostEstimate(
            flops=cost, bytes_accessed=4 * queries.size, transcendentals=queries.size
        ),
        name="attend_far",
    )(masks, far_keys, far_values, *state)


def fetch_prefix(seg_len, seg_task, task_slot, prefix_bank, t):
    grp_count = lax.axis_size("grp")
    me = lax.axis_index("grp")
    held = prefix_bank.shape[1]
    starts = jnp.cumsum(seg_len[0]) - seg_len[0]
    shards = lax.axis_index("ctx") * grp_count + jnp.arange(grp_count, dtype=jnp.int32)
    ends = shards[:, None] * t + jnp.array([0, t - 1], jnp.int32)
    segs = jnp.sum((starts[None, None, :] <= ends[:, :, None]).astype(jnp.int32), axis=2) - 1
    rows = task_slot[seg_task[0][segs]]
    local = jnp.clip(rows - me * held, 0, held - 1)
    pieces = jnp.swapaxes(prefix_bank, 0, 1)[local]
    got = lax.all_to_all(pieces, "grp", split_axis=0, concat_axis=0, tiled=True)
    owner = rows[me] // held
    return jnp.stack([got[owner[s], s] for s in range(2)])


def solution(mesh):
    in_specs = (
        P(None, AXES, None),
        P(None, None, AXES, None),
        P(),
        P(),
        P(),
        P(None, "grp", None, None),
    )
    return jax.shard_map(
        on_device, mesh=mesh, in_specs=in_specs, out_specs=P(None, AXES, None), check_vma=False
    )
```

```python
import functools
import math

import jax
import jax.numpy as jnp
from jax import lax
from jax.experimental import pallas as pl
from jax.experimental.pallas import tpu as pltpu
from jax.sharding import PartitionSpec as P

HD = 128
HOPS = 3
FAR = -1e30
AXES = ("ctx", "grp")
VMEM = pl.BlockSpec(memory_space=pltpu.VMEM)
HBM = pl.BlockSpec(memory_space=pltpu.HBM)
SCALE = math.log2(math.e) / math.sqrt(HD)
PARAMS = pltpu.CompilerParams(vmem_limit_bytes=40 * 2**20)


def shift_route(count, distance):
    return [(i, (i + distance) % count) for i in range(count)]


def flip_route(ctx_count, grp_count, flip):
    count = ctx_count * grp_count
    return [
        (i, (i + ((i % grp_count ^ flip) - i % grp_count) % grp_count) % count)
        for i in range(count)
    ]


def compose_route(wanted, first):
    holder = dict(first)
    return [(holder[s], d) for s, d in wanted]


def segments_at(len_ref, positions):
    def step(s, carry):
        start, found = carry
        out = []
        for position, (seg, begin) in zip(positions, found):
            reached = start <= position
            out.append((jnp.where(reached, s, seg), jnp.where(reached, start, begin)))
        return start + len_ref[0, s], out

    zero = jnp.int32(0)
    steps = len_ref.shape[1]
    return lax.fori_loop(0, steps, step, (zero, [(zero, zero)] * len(positions)))[1]


def block_mask(first, hop, start_a, start_b, t):
    key = lax.broadcasted_iota(jnp.int32, (t, t), 0) - hop * t
    query = lax.broadcasted_iota(jnp.int32, (t, t), 1)
    from_b = start_b - first
    start = jnp.where(query >= from_b, from_b, start_a - first)
    return jnp.where((key >= start) & (key <= query), 0.0, FAR).astype(jnp.bfloat16)


def hop_of(kind, grp_count):
    me = lax.axis_index("grp")
    if kind[0] == "shift":
        return kind[1]
    return (me - (me ^ kind[1])) & (grp_count - 1)


def plan_kernel(t, kinds, plane, len_hbm, task_hbm, slot_hbm, bank_hbm, mask_ref, *refs):
    (len_ref, task_ref, slot_ref, bank_ref, sems) = refs[-5:]
    pairs = ((len_hbm, len_ref), (task_hbm, task_ref), (slot_hbm, slot_ref), (bank_hbm, bank_ref))
    copies = [pltpu.make_async_copy(a, b, sems.at[i]) for i, (a, b) in enumerate(pairs)]
    for copy in copies:
        copy.start()
    for copy in copies[:3]:
        copy.wait()
    grp_count = lax.axis_size("grp")
    me = lax.axis_index("grp")
    row_base = lax.axis_index("ctx") * grp_count
    held = bank_ref.shape[1]
    first = (row_base + me) * t
    positions = [first, first + (t - 1)]
    groups = []
    if plane:
        across = me ^ 2
        groups = [[me, me + 1], [me ^ 1, (me ^ 1) + 1], [(across & 2) + k for k in range(3)]]
        positions += [(row_base + k) * t for group in groups for k in group]
    found = segments_at(len_ref, positions)
    (_, start_a), (_, start_b) = found[:2]
    size = bank_ref.shape[2]
    query = lax.broadcasted_iota(jnp.int32, (size, t), 1)
    from_b = start_b - first
    is_b = (query >= from_b) & (from_b > 0)
    blocks = [block_mask(first, hop_of(k, grp_count), start_a, start_b, t) for k in kinds]
    blocks[-1:-1] = [
        jnp.where(is_b, a, b).astype(jnp.bfloat16) for a, b in ((FAR, 0.0), (0.0, FAR))
    ]
    mask_ref[...] = jnp.concatenate(blocks, axis=0)
    if not plane:
        copies[3].wait()
        return
    place_ref, out_refs = refs[0], refs[1:-5]
    rows = [slot_ref[task_ref[0, seg]] for seg, _ in found[2:]]
    for i, row in enumerate(rows[:4]):
        place_ref[i] = jnp.full(place_ref.shape[1:], (row // held) ^ me, jnp.int32)
    copies[3].wait()
    for group, out_ref in zip(groups, out_refs):
        for i in range(len(group)):
            local = jnp.clip(rows.pop(0) - me * held, 0, held - 1)
            for part in range(2):
                out_ref[i, part] = bank_ref[part, local]


def here(place_ref, i, place, shape):
    return jnp.broadcast_to(place_ref[i][:1, :1] == place, shape)


def relay_kernel(place_ref, mine_ref, got_ref, out_ref):
    at = (lax.axis_index("grp") ^ 1) & 1
    for slot in range(2):
        for part in range(2):
            got = got_ref[at + slot, part]
            own = here(place_ref, 2 + slot, 0, got.shape)
            out_ref[slot, part] = jnp.where(own, mine_ref[slot, part], got)


def eye(t):
    a, b = (lax.broadcasted_iota(jnp.int32, (t, t), i) for i in range(2))
    return (a == b).astype(jnp.float32).astype(jnp.bfloat16)


def staged(count, score, weigh, mix):
    scores, weights = {}, {}
    for i in range(count + 2):
        if i < count:
            scores[i] = score(i)
        if 0 <= i - 1 < count:
            weights[i - 1] = weigh(i - 1, scores.pop(i - 1))
        if 0 <= i - 2 < count:
            mix(i - 2, weights.pop(i - 2))


def score(keys, masks, q):
    t = masks.shape[1]
    ones = jnp.concatenate([eye(t)] * (q.shape[1] // t), axis=1)
    return jnp.dot(
        jnp.concatenate([keys, masks], axis=1),
        jnp.concatenate([q, ones], axis=0),
        preferred_element_type=jnp.float32,
    )


def mix(values, weights):
    v = jnp.concatenate([values.T, jnp.ones((16, values.shape[0]), jnp.bfloat16)], axis=0)
    return jnp.dot(v, weights, preferred_element_type=jnp.float32)


def lanes(j):
    return slice(j * HD, (j + 1) * HD)


def own_kernel(groups, mask_ref, q_hbm, own_hbm, *refs):
    qt_ref, acc_ref, sum_ref, top_ref, q_ref, own_ref, q_sems, own_sem = refs
    own_copy = pltpu.make_async_copy(own_hbm, own_ref, own_sem)
    own_copy.start()
    q_copies = []
    for j in range(acc_ref.shape[0]):
        cols = pl.ds(j * groups * HD, groups * HD)
        q_copies.append(
            pltpu.make_async_copy(q_hbm.at[:, :, cols], q_ref.at[:, :, cols], q_sems.at[j])
        )
        q_copies[-1].start()
    t = q_ref.shape[1]
    masks = mask_ref[:t, :]
    own_copy.wait()

    def scored(j):
        q_copies[j].wait()
        q = jnp.concatenate([q_ref[0, :, lanes(j * groups + g)].T for g in range(groups)], axis=1)
        qt_ref[j] = q
        return score(own_ref[0, 0, :, lanes(j)], masks, q)

    def weighed(j, s):
        top = jnp.max(s, axis=0, keepdims=True) * SCALE
        top_ref[j : j + 1, :] = top
        return jnp.exp2(s * SCALE - top).astype(jnp.bfloat16)

    def mixed(j, w):
        o = mix(own_ref[1, 0, :, lanes(j)], w)
        acc_ref[j] = o[:HD]
        sum_ref[j : j + 1, :] = o[HD : HD + 1]

    staged(acc_ref.shape[0], scored, weighed, mixed)


def merge(rows, masks, qt_ref, old, finish):
    acc_ref, sum_ref, top_ref = old

    def scored(j):
        return score(rows(0, j), masks, qt_ref[j])

    def weighed(j, s):
        before = top_ref[j : j + 1, :]
        top = jnp.maximum(jnp.max(s, axis=0, keepdims=True) * SCALE, before)
        return jnp.exp2(s * SCALE - top).astype(jnp.bfloat16), jnp.exp2(before - top), top

    def mixed(j, step):
        w, keep, top = step
        o = mix(rows(1, j), w)
        finish(j, acc_ref[j], o[:HD], keep, sum_ref[j : j + 1, :] * keep + o[HD : HD + 1], top)

    staged(acc_ref.shape[0], scored, weighed, mixed)


def near_kernel(mask_ref, qt_ref, *refs):
    kv_refs, old, new = refs[:-6], refs[-6:-3], refs[-3:]
    acc_ref, sum_ref, top_ref = new
    t = mask_ref.shape[1]

    def rows(part, j):
        return jnp.concatenate([r[part, 0, :, lanes(j)] for r in kv_refs], axis=0)

    def finish(j, acc, more, keep, total, top):
        acc_ref[j] = acc * keep + more
        sum_ref[j : j + 1, :] = total
        top_ref[j : j + 1, :] = top

    merge(rows, mask_ref[t : (1 + len(kv_refs)) * t, :], qt_ref, old, finish)


def far_kernel(groups, plane, mask_ref, qt_ref, k_ref, v_ref, *refs):
    prefix_refs, old, (out_hbm, out_ref, sems) = refs[:-6], refs[-6:-3], refs[-3:]
    t = mask_ref.shape[1]
    size = prefix_refs[-1].shape[2]
    picked = [[], []]
    for part in range(2):
        for slot in range(2):
            value = prefix_refs[-1][slot, part]
            if plane:
                place_ref, own_ref, got_ref = prefix_refs[:3]
                got = got_ref[(lax.axis_index("grp") & 1) + slot, part]
                value = jnp.where(here(place_ref, slot, 2, value.shape), got, value)
                value = jnp.where(here(place_ref, slot, 0, value.shape), own_ref[slot, part], value)
            picked[part].append(value)
    copies = []

    def rows(part, j):
        block = (k_ref, v_ref)[part][0, 0, :, lanes(j)]
        return jnp.concatenate([p[:, lanes(j)] for p in picked[part]] + [block], axis=0)

    def finish(j, acc, more, keep, total, top):
        part = 1.0 / total
        done = acc * (keep * part) + more * part
        for g in range(groups):
            out_ref[0, :, lanes(j * groups + g)] = (
                done[:, g * t : (g + 1) * t].T.astype(out_ref.dtype)
            )
        cols = pl.ds(j * groups * HD, groups * HD)
        copies.append(
            pltpu.make_async_copy(out_ref.at[:, :, cols], out_hbm.at[:, :, cols], sems.at[j])
        )
        copies[-1].start()

    merge(rows, mask_ref[mask_ref.shape[0] - t - 2 * size :, :], qt_ref, old, finish)
    for copy in copies:
        copy.wait()


def on_device(queries, keyvals, seg_len, seg_task, task_slot, prefix_bank):
    ctx_count, grp_count = (lax.axis_size(a) for a in AXES)
    t = queries.shape[1]
    kv_heads = keyvals.shape[3] // HD
    groups = queries.shape[2] // keyvals.shape[3]
    plane = grp_count == HOPS + 1
    row_shape = (2,) + prefix_bank.shape[2:]
    if plane:
        kinds = [("shift", 0)] + [("flip", k) for k in range(1, HOPS + 1)]
        near, side, far = (flip_route(ctx_count, grp_count, k) for k in range(1, HOPS + 1))
    else:
        kinds = [("shift", d) for d in range(HOPS + 1)]
        near, side, far = (shift_route(ctx_count * grp_count, d) for d in range(1, HOPS + 1))

    def struct(shape, dtype):
        return jax.ShapeDtypeStruct(shape, dtype)

    def in_hbm(array):
        return pltpu.with_memory_space_constraint(array, pltpu.HBM)

    def rows_of(count):
        return struct((count,) + row_shape, prefix_bank.dtype)

    def flip(array, k):
        return lax.ppermute(array, "grp", [(i, i ^ k) for i in range(grp_count)])

    def cost(blocks):
        return pl.CostEstimate(
            flops=4 * blocks * queries.size * t,
            bytes_accessed=2 * queries.size,
            transcendentals=blocks * queries.size,
        )

    got_near = lax.ppermute(keyvals, AXES, near)
    got_side = lax.ppermute(keyvals, AXES, side)

    extra = [struct((4, 8, 128), jnp.int32)] + [rows_of(n) for n in (2, 2, 3)] if plane else []
    masks, *planned = pl.pallas_call(
        functools.partial(plan_kernel, t, kinds, plane),
        out_shape=[struct((len(kinds) * t + 2 * row_shape[1], t), jnp.bfloat16)] + extra,
        in_specs=[HBM] * 4,
        out_specs=[VMEM] * (1 + len(extra)),
        scratch_shapes=[pltpu.SMEM(a.shape, a.dtype) for a in (seg_len, seg_task, task_slot)]
        + [pltpu.VMEM(prefix_bank.shape, prefix_bank.dtype), pltpu.SemaphoreType.DMA((4,))],
        compiler_params=PARAMS,
        name="plan",
    )(*(in_hbm(a) for a in (seg_len, seg_task, task_slot, prefix_bank)))

    wide = struct((kv_heads, HD, groups * t), jnp.float32)
    flat = struct((kv_heads, groups * t), jnp.float32)
    turned, *state = pl.pallas_call(
        functools.partial(own_kernel, groups),
        out_shape=[struct(wide.shape, queries.dtype), wide, flat, flat],
        in_specs=[VMEM, HBM, HBM],
        out_specs=[VMEM] * 4,
        scratch_shapes=[
            pltpu.VMEM(queries.shape, queries.dtype),
            pltpu.VMEM(keyvals.shape, keyvals.dtype),
            pltpu.SemaphoreType.DMA((kv_heads,)),
            pltpu.SemaphoreType.DMA,
        ],
        compiler_params=PARAMS,
        cost_estimate=cost(1),
        name="attend_own",
    )(masks, in_hbm(queries), in_hbm(keyvals))

    if plane:
        place, own_rows, near_rows, side_rows = planned
        got_rows = flip(side_rows, 2)
        ready, _ = lax.optimization_barrier((got_side, state[-1]))
        far_keys = lax.ppermute(ready[0:1], AXES, compose_route(far, side))
        far_values = lax.ppermute(got_near[1:2], AXES, compose_route(far, near))
        relayed = pl.pallas_call(
            relay_kernel,
            out_shape=rows_of(2),
            in_specs=[VMEM] * 3,
            out_specs=VMEM,
            compiler_params=PARAMS,
            name="relay_rows",
        )(place, near_rows, got_rows)
        prefix = [place, own_rows, got_rows, flip(relayed, 1)]
    else:
        prefix = [fetch_prefix(seg_len, seg_task, task_slot, prefix_bank, t)]
        got_far = lax.ppermute(keyvals, AXES, far)
        far_keys, far_values = got_far[0:1], got_far[1:2]

    state = pl.pallas_call(
        near_kernel,
        out_shape=[wide, flat, flat],
        in_specs=[VMEM] * 7,
        out_specs=[VMEM] * 3,
        compiler_params=PARAMS,
        cost_estimate=cost(2),
        name="attend_near",
    )(masks, turned, got_near, got_side, *state)
    return pl.pallas_call(
        functools.partial(far_kernel, groups, plane),
        out_shape=struct(queries.shape, queries.dtype),
        in_specs=[VMEM] * (7 + len(prefix)),
        out_specs=HBM,
        scratch_shapes=[
            pltpu.VMEM(queries.shape, queries.dtype),
            pltpu.SemaphoreType.DMA((kv_heads,)),
        ],
        compiler_params=PARAMS,
        cost_estimate=cost(1),
        name="attend_far",
    )(masks, turned, far_keys, far_values, *prefix, *state)


def fetch_prefix(seg_len, seg_task, task_slot, prefix_bank, t):
    grp_count = lax.axis_size("grp")
    me = lax.axis_index("grp")
    held = prefix_bank.shape[1]
    starts = jnp.cumsum(seg_len[0]) - seg_len[0]
    shards = lax.axis_index("ctx") * grp_count + jnp.arange(grp_count, dtype=jnp.int32)
    ends = shards[:, None] * t + jnp.array([0, t - 1], jnp.int32)
    segs = jnp.sum((starts[None, None, :] <= ends[:, :, None]).astype(jnp.int32), axis=2) - 1
    rows = task_slot[seg_task[0][segs]]
    local = jnp.clip(rows - me * held, 0, held - 1)
    pieces = jnp.swapaxes(prefix_bank, 0, 1)[local]
    got = lax.all_to_all(pieces, "grp", split_axis=0, concat_axis=0, tiled=True)
    owner = rows[me] // held
    return jnp.stack([got[owner[s], s] for s in range(2)])


def solution(mesh):
    in_specs = (
        P(None, AXES, None),
        P(None, None, AXES, None),
        P(),
        P(),
        P(),
        P(None, "grp", None, None),
    )
    return jax.shard_map(
        on_device, mesh=mesh, in_specs=in_specs, out_specs=P(None, AXES, None), check_vma=False
    )
```

```python
import functools
import math

import jax
import jax.numpy as jnp
from jax import lax
from jax.experimental import pallas as pl
from jax.experimental.pallas import tpu as pltpu
from jax.sharding import PartitionSpec as P

HD = 128
HOPS = 3
FAR = -1e30
AXES = ("ctx", "grp")
VMEM = pl.BlockSpec(memory_space=pltpu.VMEM)
HBM = pl.BlockSpec(memory_space=pltpu.HBM)
SCALE = math.log2(math.e) / math.sqrt(HD)
PARAMS = pltpu.CompilerParams(vmem_limit_bytes=40 * 2**20)


def shift_route(count, distance):
    return [(i, (i + distance) % count) for i in range(count)]


def flip_route(ctx_count, grp_count, flip):
    count = ctx_count * grp_count
    return [
        (i, (i + ((i % grp_count ^ flip) - i % grp_count) % grp_count) % count)
        for i in range(count)
    ]


def compose_route(wanted, first):
    holder = dict(first)
    return [(holder[s], d) for s, d in wanted]


def segments_at(len_ref, positions):
    def step(s, carry):
        start, found = carry
        out = []
        for position, (seg, begin) in zip(positions, found):
            reached = start <= position
            out.append((jnp.where(reached, s, seg), jnp.where(reached, start, begin)))
        return start + len_ref[0, s], out

    zero = jnp.int32(0)
    steps = len_ref.shape[1]
    return lax.fori_loop(0, steps, step, (zero, [(zero, zero)] * len(positions)))[1]


def block_mask(first, hop, start_a, start_b, t):
    key = lax.broadcasted_iota(jnp.int32, (t, t), 0) - hop * t
    query = lax.broadcasted_iota(jnp.int32, (t, t), 1)
    from_b = start_b - first
    start = jnp.where(query >= from_b, from_b, start_a - first)
    return jnp.where((key >= start) & (key <= query), 0.0, FAR).astype(jnp.bfloat16)


def hop_of(kind, grp_count):
    me = lax.axis_index("grp")
    if kind[0] == "shift":
        return kind[1]
    return (me - (me ^ kind[1])) & (grp_count - 1)


def plan_kernel(
    t,
    kinds,
    plane,
    len_hbm,
    task_hbm,
    slot_hbm,
    bank_hbm,
    kv_hbm,
    q_hbm,
    mask_ref,
    k_ref,
    v_ref,
    q_ref,
    *refs,
):
    (len_ref, task_ref, slot_ref, bank_ref, sems) = refs[-5:]
    pairs = (
        (len_hbm, len_ref),
        (task_hbm, task_ref),
        (slot_hbm, slot_ref),
        (kv_hbm.at[pl.ds(0, 1)], k_ref),
        (kv_hbm.at[pl.ds(1, 1)], v_ref),
        (bank_hbm, bank_ref),
        (q_hbm, q_ref),
    )
    copies = [pltpu.make_async_copy(a, b, sems.at[i]) for i, (a, b) in enumerate(pairs)]
    for copy in copies:
        copy.start()
    for copy in copies[:3]:
        copy.wait()
    grp_count = lax.axis_size("grp")
    me = lax.axis_index("grp")
    row_base = lax.axis_index("ctx") * grp_count
    held = bank_ref.shape[1]
    first = (row_base + me) * t
    positions = [first, first + (t - 1)]
    groups = []
    if plane:
        across = me ^ 2
        groups = [[me, me + 1], [me ^ 1, (me ^ 1) + 1], [(across & 2) + k for k in range(3)]]
        positions += [(row_base + k) * t for group in groups for k in group]
    found = segments_at(len_ref, positions)
    (_, start_a), (_, start_b) = found[:2]
    size = bank_ref.shape[2]
    query = lax.broadcasted_iota(jnp.int32, (size, t), 1)
    from_b = start_b - first
    is_b = (query >= from_b) & (from_b > 0)
    blocks = [block_mask(first, hop_of(k, grp_count), start_a, start_b, t) for k in kinds]
    blocks[-1:-1] = [
        jnp.where(is_b, a, b).astype(jnp.bfloat16) for a, b in ((FAR, 0.0), (0.0, FAR))
    ]
    mask_ref[...] = jnp.concatenate(blocks, axis=0)
    for copy in copies[3:6]:
        copy.wait()
    if not plane:
        copies[6].wait()
        return
    place_ref, out_refs = refs[0], refs[1:-5]
    rows = [slot_ref[task_ref[0, seg]] for seg, _ in found[2:]]
    for i, row in enumerate(rows[:4]):
        place_ref[i] = jnp.full(place_ref.shape[1:], (row // held) ^ me, jnp.int32)
    for group, out_ref in zip(groups, out_refs):
        for i in range(len(group)):
            local = jnp.clip(rows.pop(0) - me * held, 0, held - 1)
            for part in range(2):
                out_ref[i, part] = bank_ref[part, local]
    copies[6].wait()


def here(place_ref, i, place, shape):
    return jnp.broadcast_to(place_ref[i][:1, :1] == place, shape)


def relay_kernel(place_ref, mine_ref, got_ref, out_ref):
    at = (lax.axis_index("grp") ^ 1) & 1
    for slot in range(2):
        for part in range(2):
            got = got_ref[at + slot, part]
            own = here(place_ref, 2 + slot, 0, got.shape)
            out_ref[slot, part] = jnp.where(own, mine_ref[slot, part], got)


def eye(t):
    a, b = (lax.broadcasted_iota(jnp.int32, (t, t), i) for i in range(2))
    return (a == b).astype(jnp.float32).astype(jnp.bfloat16)


def staged(count, score, weigh, mix):
    scores, weights = {}, {}
    for i in range(count + 2):
        if i < count:
            scores[i] = score(i)
        if 0 <= i - 1 < count:
            weights[i - 1] = weigh(i - 1, scores.pop(i - 1))
        if 0 <= i - 2 < count:
            mix(i - 2, weights.pop(i - 2))


def score(keys, masks, q):
    t = masks.shape[1]
    ones = jnp.concatenate([eye(t)] * (q.shape[1] // t), axis=1)
    return jnp.dot(
        jnp.concatenate([keys, masks], axis=1),
        jnp.concatenate([q, ones], axis=0),
        preferred_element_type=jnp.float32,
    )


def mix(values, weights):
    v = jnp.concatenate([values.T, jnp.ones((16, values.shape[0]), jnp.bfloat16)], axis=0)
    return jnp.dot(v, weights, preferred_element_type=jnp.float32)


def lanes(j):
    return slice(j * HD, (j + 1) * HD)


def near_kernel(groups, mask_ref, q_ref, *refs):
    kv_refs, (qt_ref, acc_ref, sum_ref, top_ref) = refs[:-4], refs[-4:]
    masks = mask_ref[: len(kv_refs) // 2 * q_ref.shape[1], :]

    def rows(part, j):
        return jnp.concatenate([r[0, 0, :, lanes(j)] for r in kv_refs[part::2]], axis=0)

    def scored(j):
        q = jnp.concatenate([q_ref[0, :, lanes(j * groups + g)].T for g in range(groups)], axis=1)
        qt_ref[j] = q
        return score(rows(0, j), masks, q)

    def weighed(j, s):
        top = jnp.max(s, axis=0, keepdims=True) * SCALE
        top_ref[j : j + 1, :] = top
        return jnp.exp2(s * SCALE - top).astype(jnp.bfloat16)

    def mixed(j, w):
        o = mix(rows(1, j), w)
        acc_ref[j] = o[:HD]
        sum_ref[j : j + 1, :] = o[HD : HD + 1]

    staged(acc_ref.shape[0], scored, weighed, mixed)


def merge(rows, masks, qt_ref, old, finish):
    acc_ref, sum_ref, top_ref = old

    def scored(j):
        return score(rows(0, j), masks, qt_ref[j])

    def weighed(j, s):
        before = top_ref[j : j + 1, :]
        top = jnp.maximum(jnp.max(s, axis=0, keepdims=True) * SCALE, before)
        return jnp.exp2(s * SCALE - top).astype(jnp.bfloat16), jnp.exp2(before - top), top

    def mixed(j, step):
        w, keep, top = step
        o = mix(rows(1, j), w)
        finish(j, acc_ref[j], o[:HD], keep, sum_ref[j : j + 1, :] * keep + o[HD : HD + 1], top)

    staged(acc_ref.shape[0], scored, weighed, mixed)


def far_kernel(groups, plane, mask_ref, qt_ref, k_ref, v_ref, *refs):
    prefix_refs, old, (out_hbm, out_ref, sems) = refs[:-6], refs[-6:-3], refs[-3:]
    t = mask_ref.shape[1]
    size = prefix_refs[-1].shape[2]
    picked = [[], []]
    for part in range(2):
        for slot in range(2):
            value = prefix_refs[-1][slot, part]
            if plane:
                place_ref, own_ref, got_ref = prefix_refs[:3]
                got = got_ref[(lax.axis_index("grp") & 1) + slot, part]
                value = jnp.where(here(place_ref, slot, 2, value.shape), got, value)
                value = jnp.where(here(place_ref, slot, 0, value.shape), own_ref[slot, part], value)
            picked[part].append(value)
    copies = []

    def rows(part, j):
        block = (k_ref, v_ref)[part][0, 0, :, lanes(j)]
        return jnp.concatenate([p[:, lanes(j)] for p in picked[part]] + [block], axis=0)

    def finish(j, acc, more, keep, total, top):
        part = 1.0 / total
        done = acc * (keep * part) + more * part
        for g in range(groups):
            out_ref[0, :, lanes(j * groups + g)] = (
                done[:, g * t : (g + 1) * t].T.astype(out_ref.dtype)
            )
        cols = pl.ds(j * groups * HD, groups * HD)
        copies.append(
            pltpu.make_async_copy(out_ref.at[:, :, cols], out_hbm.at[:, :, cols], sems.at[j])
        )
        copies[-1].start()

    merge(rows, mask_ref[mask_ref.shape[0] - t - 2 * size :, :], qt_ref, old, finish)
    for copy in copies:
        copy.wait()


def on_device(queries, keyvals, seg_len, seg_task, task_slot, prefix_bank):
    ctx_count, grp_count = (lax.axis_size(a) for a in AXES)
    t = queries.shape[1]
    kv_heads = keyvals.shape[3] // HD
    groups = queries.shape[2] // keyvals.shape[3]
    plane = grp_count == HOPS + 1
    row_shape = (2,) + prefix_bank.shape[2:]
    if plane:
        kinds = [("shift", 0)] + [("flip", k) for k in range(1, HOPS + 1)]
        near, side, far = (flip_route(ctx_count, grp_count, k) for k in range(1, HOPS + 1))
    else:
        kinds = [("shift", d) for d in range(HOPS + 1)]
        near, side, far = (shift_route(ctx_count * grp_count, d) for d in range(1, HOPS + 1))

    def struct(shape, dtype):
        return jax.ShapeDtypeStruct(shape, dtype)

    def in_hbm(array):
        return pltpu.with_memory_space_constraint(array, pltpu.HBM)

    def rows_of(count):
        return struct((count,) + row_shape, prefix_bank.dtype)

    def flip(array, k):
        return lax.ppermute(array, "grp", [(i, i ^ k) for i in range(grp_count)])

    def cost(blocks):
        return pl.CostEstimate(
            flops=4 * blocks * queries.size * t,
            bytes_accessed=2 * queries.size,
            transcendentals=blocks * queries.size,
        )

    extra = [struct((4, 8, 128), jnp.int32)] + [rows_of(n) for n in (2, 2, 3)] if plane else []
    half = struct((1,) + keyvals.shape[1:], keyvals.dtype)
    masks, keys, values, fetched, *planned = pl.pallas_call(
        functools.partial(plan_kernel, t, kinds, plane),
        out_shape=[struct((len(kinds) * t + 2 * row_shape[1], t), jnp.bfloat16)] + [half] * 2 + [struct(queries.shape, queries.dtype)] + extra,
        in_specs=[HBM] * 6,
        out_specs=[VMEM] * (4 + len(extra)),
        scratch_shapes=[pltpu.SMEM(a.shape, a.dtype) for a in (seg_len, seg_task, task_slot)]
        + [pltpu.VMEM(prefix_bank.shape, prefix_bank.dtype), pltpu.SemaphoreType.DMA((7,))],
        compiler_params=PARAMS,
        name="plan",
    )(*(in_hbm(a) for a in (seg_len, seg_task, task_slot, prefix_bank, keyvals, queries)))

    side_keys = lax.ppermute(keys, AXES, side)
    near_values = lax.ppermute(values, AXES, near)
    if plane:
        place, own_rows, near_rows, side_rows = planned
        got_rows = flip(side_rows, 2)
    near_keys = lax.ppermute(keys, AXES, near)
    side_values = lax.ppermute(values, AXES, side)
    if plane:
        far_keys = lax.ppermute(side_keys, AXES, compose_route(far, side))
        far_values = lax.ppermute(near_values, AXES, compose_route(far, near))
        relayed = pl.pallas_call(
            relay_kernel,
            out_shape=rows_of(2),
            in_specs=[VMEM] * 3,
            out_specs=VMEM,
            compiler_params=PARAMS,
            cost_estimate=cost(16),
            name="relay_rows",
        )(place, near_rows, got_rows)
        prefix = [place, own_rows, got_rows, flip(relayed, 1)]
    else:
        prefix = [fetch_prefix(seg_len, seg_task, task_slot, prefix_bank, t)]
        far_keys = lax.ppermute(keys, AXES, far)
        far_values = lax.ppermute(values, AXES, far)

    wide = struct((kv_heads, HD, groups * t), jnp.float32)
    flat = struct((kv_heads, groups * t), jnp.float32)
    kv = [keys, values, near_keys, near_values, side_keys, side_values]
    turned, *state = pl.pallas_call(
        functools.partial(near_kernel, groups),
        out_shape=[struct(wide.shape, queries.dtype), wide, flat, flat],
        in_specs=[VMEM] * (2 + len(kv)),
        out_specs=[VMEM] * 4,
        compiler_params=PARAMS,
        cost_estimate=cost(3),
        name="attend_near",
    )(masks, fetched, *kv)
    return pl.pallas_call(
        functools.partial(far_kernel, groups, plane),
        out_shape=struct(queries.shape, queries.dtype),
        in_specs=[VMEM] * (7 + len(prefix)),
        out_specs=HBM,
        scratch_shapes=[
            pltpu.VMEM(queries.shape, queries.dtype),
            pltpu.SemaphoreType.DMA((kv_heads,)),
        ],
        compiler_params=PARAMS,
        cost_estimate=cost(1),
        name="attend_far",
    )(masks, turned, far_keys, far_values, *prefix, *state)


def fetch_prefix(seg_len, seg_task, task_slot, prefix_bank, t):
    grp_count = lax.axis_size("grp")
    me = lax.axis_index("grp")
    held = prefix_bank.shape[1]
    starts = jnp.cumsum(seg_len[0]) - seg_len[0]
    shards = lax.axis_index("ctx") * grp_count + jnp.arange(grp_count, dtype=jnp.int32)
    ends = shards[:, None] * t + jnp.array([0, t - 1], jnp.int32)
    segs = jnp.sum((starts[None, None, :] <= ends[:, :, None]).astype(jnp.int32), axis=2) - 1
    rows = task_slot[seg_task[0][segs]]
    local = jnp.clip(rows - me * held, 0, held - 1)
    pieces = jnp.swapaxes(prefix_bank, 0, 1)[local]
    got = lax.all_to_all(pieces, "grp", split_axis=0, concat_axis=0, tiled=True)
    owner = rows[me] // held
    return jnp.stack([got[owner[s], s] for s in range(2)])


def solution(mesh):
    in_specs = (
        P(None, AXES, None),
        P(None, None, AXES, None),
        P(),
        P(),
        P(),
        P(None, "grp", None, None),
    )
    return jax.shard_map(
        on_device, mesh=mesh, in_specs=in_specs, out_specs=P(None, AXES, None), check_vma=False
    )
```

```python
import functools
import math

import jax
import jax.numpy as jnp
from jax import lax
from jax.experimental import pallas as pl
from jax.experimental.pallas import tpu as pltpu
from jax.sharding import PartitionSpec as P

HD = 128
HOPS = 3
FAR = -1e30
AXES = ("ctx", "grp")
VMEM = pl.BlockSpec(memory_space=pltpu.VMEM)
HBM = pl.BlockSpec(memory_space=pltpu.HBM)
SCALE = math.log2(math.e) / math.sqrt(HD)
PARAMS = pltpu.CompilerParams(vmem_limit_bytes=40 * 2**20)


def shift_route(count, distance):
    return [(i, (i + distance) % count) for i in range(count)]


def flip_route(ctx_count, grp_count, flip):
    count = ctx_count * grp_count
    return [
        (i, (i + ((i % grp_count ^ flip) - i % grp_count) % grp_count) % count)
        for i in range(count)
    ]


def compose_route(wanted, first):
    holder = dict(first)
    return [(holder[s], d) for s, d in wanted]


def segments_at(len_ref, positions, starts_of):
    steps = len_ref.shape[1]
    unroll = math.gcd(steps, 16)

    def step(block, carry):
        start, segs, begins = carry
        for k in range(unroll):
            s = block * unroll + k
            reached = [start <= position for position in positions]
            segs = [jnp.where(r, s, seg) for r, seg in zip(reached, segs)]
            begins = [jnp.where(r, start, begin) for r, begin in zip(reached, begins)]
            start = start + len_ref[0, s]
        return start, segs, begins

    zero = jnp.int32(0)
    carry = (zero, [zero] * len(positions), [zero] * starts_of)
    _, segs, begins = lax.fori_loop(0, steps // unroll, step, carry)
    return segs, begins


def block_mask(shape, hop, from_a, from_b):
    key = lax.broadcasted_iota(jnp.int32, shape, 0) - hop * shape[0]
    query = lax.broadcasted_iota(jnp.int32, shape, 1)
    start = jnp.where(query >= from_b, from_b, from_a)
    return jnp.where((key >= start) & (key <= query), 0.0, FAR).astype(jnp.bfloat16)


def all_masks(kinds, t, size, place_ref):
    from_a, from_b = (place_ref[i][:1, :1] for i in (4, 5))
    grp_count = lax.axis_size("grp")
    ends = [jnp.broadcast_to(x, (t, t)) for x in (from_a, from_b)]
    blocks = [block_mask((t, t), hop_of(k, grp_count), *ends) for k in kinds]
    b = jnp.broadcast_to(from_b, (size, t))
    is_b = (lax.broadcasted_iota(jnp.int32, (size, t), 1) >= b) & (b > 0)
    blocks[-1:-1] = [
        jnp.where(is_b, x, y).astype(jnp.bfloat16) for x, y in ((FAR, 0.0), (0.0, FAR))
    ]
    return blocks


def hop_of(kind, grp_count):
    me = lax.axis_index("grp")
    if kind[0] == "shift":
        return kind[1]
    return (me - (me ^ kind[1])) & (grp_count - 1)


def plan_kernel(t, plane, *refs):
    len_hbm, task_hbm, slot_hbm, bank_hbm, kv_hbm = refs[:5]
    place_ref, k_ref, v_ref = refs[5:8]
    out_refs = refs[8:-5]
    len_ref, task_ref, slot_ref, bank_ref, sems = refs[-5:]
    pairs = (
        (len_hbm, len_ref),
        (task_hbm, task_ref),
        (slot_hbm, slot_ref),
        (bank_hbm, bank_ref),
        (kv_hbm.at[pl.ds(0, 1)], k_ref),
        (kv_hbm.at[pl.ds(1, 1)], v_ref),
    )
    copies = [pltpu.make_async_copy(x, y, sems.at[i]) for i, (x, y) in enumerate(pairs)]
    for copy in copies:
        copy.start()
    for copy in copies[:3]:
        copy.wait()
    grp_count = lax.axis_size("grp")
    me = lax.axis_index("grp")
    row_base = lax.axis_index("ctx") * grp_count
    held = bank_ref.shape[1]
    first = (row_base + me) * t
    positions = [first, first + (t - 1)]
    groups = []
    if plane:
        across = me ^ 2
        groups = [[me, me + 1], [me ^ 1, (me ^ 1) + 1], [(across & 2) + k for k in range(3)]]
        positions += [(row_base + k) * t for group in groups for k in group]
    segs, begins = segments_at(len_ref, positions, 2)
    for i, begin in enumerate(begins):
        place_ref[4 + i] = jnp.full(place_ref.shape[1:], begin - first, jnp.int32)
    if plane:
        rows = [slot_ref[task_ref[0, seg]] for seg in segs[2:]]
        for i, row in enumerate(rows[:4]):
            place_ref[i] = jnp.full(place_ref.shape[1:], (row // held) ^ me, jnp.int32)
        copies[3].wait()
        for group, out_ref in zip(groups, out_refs):
            for i in range(len(group)):
                local = jnp.clip(rows.pop(0) - me * held, 0, held - 1)
                for part in range(2):
                    out_ref[i, part] = bank_ref[part, local]
    for copy in copies[4 if plane else 3 :]:
        copy.wait()


def here(place_ref, i, place, shape):
    return jnp.broadcast_to(place_ref[i][:1, :1] == place, shape)


def pass_kernel(in_ref, out_ref):
    out_ref[...] = in_ref[...]


def relay_kernel(place_ref, mine_ref, got_ref, out_ref):
    at = (lax.axis_index("grp") ^ 1) & 1
    for slot in range(2):
        for part in range(2):
            got = got_ref[at + slot, part]
            own = here(place_ref, 2 + slot, 0, got.shape)
            out_ref[slot, part] = jnp.where(own, mine_ref[slot, part], got)


def eye(t):
    a, b = (lax.broadcasted_iota(jnp.int32, (t, t), i) for i in range(2))
    return (a == b).astype(jnp.float32).astype(jnp.bfloat16)


def staged(count, score, weigh, mix):
    scores, weights = {}, {}
    for i in range(count + 2):
        if i < count:
            scores[i] = score(i)
        if 0 <= i - 1 < count:
            weights[i - 1] = weigh(i - 1, scores.pop(i - 1))
        if 0 <= i - 2 < count:
            mix(i - 2, weights.pop(i - 2))


def score(keys, masks, q):
    t = masks.shape[1]
    ones = jnp.concatenate([eye(t)] * (q.shape[1] // t), axis=1)
    return jnp.dot(
        jnp.concatenate([keys, masks], axis=1),
        jnp.concatenate([q, ones], axis=0),
        preferred_element_type=jnp.float32,
    )


def mix(values, weights):
    v = jnp.concatenate([values.T, jnp.ones((16, values.shape[0]), jnp.bfloat16)], axis=0)
    return jnp.dot(v, weights, preferred_element_type=jnp.float32)


def lanes(j):
    return slice(j * HD, (j + 1) * HD)


def own_kernel(groups, kinds, size, place_ref, q_hbm, k_ref, v_ref, *refs):
    mask_ref, qt_ref, acc_ref, sum_ref, top_ref, q_ref, sem = refs
    copy = pltpu.make_async_copy(q_hbm, q_ref, sem)
    copy.start()
    t = q_ref.shape[1]
    blocks = all_masks(kinds, t, size, place_ref)
    mask_ref[...] = jnp.concatenate(blocks, axis=0)
    copy.wait()

    def scored(j):
        q = jnp.concatenate([q_ref[0, :, lanes(j * groups + g)].T for g in range(groups)], axis=1)
        qt_ref[j] = q
        return score(k_ref[0, 0, :, lanes(j)], blocks[0], q)

    def weighed(j, s):
        top = jnp.max(s, axis=0, keepdims=True) * SCALE
        top_ref[j : j + 1, :] = top
        return jnp.exp2(s * SCALE - top).astype(jnp.bfloat16)

    def mixed(j, w):
        o = mix(v_ref[0, 0, :, lanes(j)], w)
        acc_ref[j] = o[:HD]
        sum_ref[j : j + 1, :] = o[HD : HD + 1]

    staged(acc_ref.shape[0], scored, weighed, mixed)


def merge(rows, masks, qt_ref, old, finish):
    acc_ref, sum_ref, top_ref = old

    def scored(j):
        return score(rows(0, j), masks, qt_ref[j])

    def weighed(j, s):
        before = top_ref[j : j + 1, :]
        top = jnp.maximum(jnp.max(s, axis=0, keepdims=True) * SCALE, before)
        return jnp.exp2(s * SCALE - top).astype(jnp.bfloat16), jnp.exp2(before - top), top

    def mixed(j, step):
        w, keep, top = step
        o = mix(rows(1, j), w)
        finish(j, acc_ref[j], o[:HD], keep, sum_ref[j : j + 1, :] * keep + o[HD : HD + 1], top)

    staged(acc_ref.shape[0], scored, weighed, mixed)


def near_kernel(mask_ref, qt_ref, *refs):
    kv_refs, old, new = refs[:-6], refs[-6:-3], refs[-3:]
    acc_ref, sum_ref, top_ref = new
    t = mask_ref.shape[1]
    count = len(kv_refs) // 2

    def rows(part, j):
        return jnp.concatenate([r[0, 0, :, lanes(j)] for r in kv_refs[part::2]], axis=0)

    def finish(j, acc, more, keep, total, top):
        acc_ref[j] = acc * keep + more
        sum_ref[j : j + 1, :] = total
        top_ref[j : j + 1, :] = top

    merge(rows, mask_ref[t : (1 + count) * t, :], qt_ref, old, finish)


def far_kernel(groups, plane, mask_ref, qt_ref, k_ref, v_ref, *refs):
    prefix_refs, old, (out_hbm, out_ref, sems) = refs[:-6], refs[-6:-3], refs[-3:]
    t = mask_ref.shape[1]
    size = prefix_refs[-1].shape[2]
    picked = [[], []]
    for part in range(2):
        for slot in range(2):
            value = prefix_refs[-1][slot, part]
            if plane:
                place_ref, own_ref, got_ref = prefix_refs[:3]
                got = got_ref[(lax.axis_index("grp") & 1) + slot, part]
                value = jnp.where(here(place_ref, slot, 2, value.shape), got, value)
                value = jnp.where(here(place_ref, slot, 0, value.shape), own_ref[slot, part], value)
            picked[part].append(value)
    copies = []

    def rows(part, j):
        block = (k_ref, v_ref)[part][0, 0, :, lanes(j)]
        return jnp.concatenate([p[:, lanes(j)] for p in picked[part]] + [block], axis=0)

    def finish(j, acc, more, keep, total, top):
        part = 1.0 / total
        done = acc * (keep * part) + more * part
        for g in range(groups):
            out_ref[0, :, lanes(j * groups + g)] = (
                done[:, g * t : (g + 1) * t].T.astype(out_ref.dtype)
            )
        cols = pl.ds(j * groups * HD, groups * HD)
        copies.append(
            pltpu.make_async_copy(out_ref.at[:, :, cols], out_hbm.at[:, :, cols], sems.at[j])
        )
        copies[-1].start()

    merge(rows, mask_ref[mask_ref.shape[0] - t - 2 * size :, :], qt_ref, old, finish)
    for copy in copies:
        copy.wait()


def on_device(queries, keyvals, seg_len, seg_task, task_slot, prefix_bank):
    ctx_count, grp_count = (lax.axis_size(a) for a in AXES)
    t = queries.shape[1]
    kv_heads = keyvals.shape[3] // HD
    groups = queries.shape[2] // keyvals.shape[3]
    plane = grp_count == HOPS + 1
    row_shape = (2,) + prefix_bank.shape[2:]
    if plane:
        kinds = [("shift", 0)] + [("flip", k) for k in range(1, HOPS + 1)]
        near, side, far = (flip_route(ctx_count, grp_count, k) for k in range(1, HOPS + 1))
    else:
        kinds = [("shift", d) for d in range(HOPS + 1)]
        near, side, far = (shift_route(ctx_count * grp_count, d) for d in range(1, HOPS + 1))

    def struct(shape, dtype):
        return jax.ShapeDtypeStruct(shape, dtype)

    def in_hbm(array):
        return pltpu.with_memory_space_constraint(array, pltpu.HBM)

    def rows_of(count):
        return struct((count,) + row_shape, prefix_bank.dtype)

    def flip(array, k):
        return lax.ppermute(array, "grp", [(i, i ^ k) for i in range(grp_count)])

    def cost(quarters):
        return pl.CostEstimate(
            flops=quarters * queries.size * t,
            bytes_accessed=quarters * queries.size // 2,
            transcendentals=quarters * queries.size // 4,
        )

    extra = [struct((4, 8, 128), jnp.int32)] + [rows_of(n) for n in (2, 2, 3)] if plane else []
    half = struct((1,) + keyvals.shape[1:], keyvals.dtype)
    arguments = (seg_len, seg_task, task_slot, prefix_bank, keyvals)
    outputs = [struct((6, 8, 128), jnp.int32), half, half]
    outputs += [rows_of(n) for n in (2, 2, 3)] if plane else []
    place, keys, values, *planned = pl.pallas_call(
        functools.partial(plan_kernel, t, plane),
        out_shape=outputs,
        in_specs=[HBM] * len(arguments),
        out_specs=[VMEM] * len(outputs),
        scratch_shapes=[pltpu.SMEM(a.shape, a.dtype) for a in arguments[:3]]
        + [pltpu.VMEM(prefix_bank.shape, prefix_bank.dtype), pltpu.SemaphoreType.DMA((6,))],
        compiler_params=PARAMS,
        name="plan",
    )(*(in_hbm(a) for a in arguments))

    side_keys = lax.ppermute(keys, AXES, side)
    near_values = lax.ppermute(values, AXES, near)
    if plane:
        own_rows, near_rows, side_rows = planned
        got_rows = flip(side_rows, 2)
    near_keys = lax.ppermute(keys, AXES, near)
    side_values = lax.ppermute(values, AXES, side)
    if plane:
        far_keys = lax.ppermute(side_keys, AXES, compose_route(far, side))
        far_values = lax.ppermute(near_values, AXES, compose_route(far, near))
        relayed = pl.pallas_call(
            relay_kernel,
            out_shape=rows_of(2),
            in_specs=[VMEM] * 3,
            out_specs=VMEM,
            compiler_params=PARAMS,
            cost_estimate=cost(32),
            name="relay_rows",
        )(place, near_rows, got_rows)
        relayed = pl.pallas_call(
            pass_kernel,
            out_shape=rows_of(2),
            in_specs=[VMEM],
            out_specs=VMEM,
            compiler_params=PARAMS,
            cost_estimate=cost(4),
            name="settle",
        )(flip(relayed, 1))
        prefix = [place, own_rows, got_rows, relayed]
    else:
        prefix = [fetch_prefix(seg_len, seg_task, task_slot, prefix_bank, t)]
        far_keys = lax.ppermute(keys, AXES, far)
        far_values = lax.ppermute(values, AXES, far)

    wide = struct((kv_heads, HD, groups * t), jnp.float32)
    flat = struct((kv_heads, groups * t), jnp.float32)
    masks, turned, *state = pl.pallas_call(
        functools.partial(own_kernel, groups, kinds, row_shape[1]),
        out_shape=[
            struct((len(kinds) * t + 2 * row_shape[1], t), jnp.bfloat16),
            struct(wide.shape, queries.dtype),
            wide,
            flat,
            flat,
        ],
        in_specs=[VMEM, HBM, VMEM, VMEM],
        out_specs=[VMEM] * 5,
        scratch_shapes=[pltpu.VMEM(queries.shape, queries.dtype), pltpu.SemaphoreType.DMA],
        compiler_params=PARAMS,
        cost_estimate=cost(8),
        name="attend_own",
    )(place, in_hbm(queries), keys, values)
    state = pl.pallas_call(
        near_kernel,
        out_shape=[wide, flat, flat],
        in_specs=[VMEM] * 9,
        out_specs=[VMEM] * 3,
        compiler_params=PARAMS,
        cost_estimate=cost(2),
        name="attend_near",
    )(masks, turned, near_keys, near_values, side_keys, side_values, *state)
    return pl.pallas_call(
        functools.partial(far_kernel, groups, plane),
        out_shape=struct(queries.shape, queries.dtype),
        in_specs=[VMEM] * (7 + len(prefix)),
        out_specs=HBM,
        scratch_shapes=[
            pltpu.VMEM(queries.shape, queries.dtype),
            pltpu.SemaphoreType.DMA((kv_heads,)),
        ],
        compiler_params=PARAMS,
        cost_estimate=cost(4),
        name="attend_far",
    )(masks, turned, far_keys, far_values, *prefix, *state)


def fetch_prefix(seg_len, seg_task, task_slot, prefix_bank, t):
    grp_count = lax.axis_size("grp")
    me = lax.axis_index("grp")
    held = prefix_bank.shape[1]
    starts = jnp.cumsum(seg_len[0]) - seg_len[0]
    shards = lax.axis_index("ctx") * grp_count + jnp.arange(grp_count, dtype=jnp.int32)
    ends = shards[:, None] * t + jnp.array([0, t - 1], jnp.int32)
    segs = jnp.sum((starts[None, None, :] <= ends[:, :, None]).astype(jnp.int32), axis=2) - 1
    rows = task_slot[seg_task[0][segs]]
    local = jnp.clip(rows - me * held, 0, held - 1)
    pieces = jnp.swapaxes(prefix_bank, 0, 1)[local]
    got = lax.all_to_all(pieces, "grp", split_axis=0, concat_axis=0, tiled=True)
    owner = rows[me] // held
    return jnp.stack([got[owner[s], s] for s in range(2)])


def solution(mesh):
    in_specs = (
        P(None, AXES, None),
        P(None, None, AXES, None),
        P(),
        P(),
        P(),
        P(None, "grp", None, None),
    )
    return jax.shard_map(
        on_device, mesh=mesh, in_specs=in_specs, out_specs=P(None, AXES, None), check_vma=False
    )
```

```python
import functools
import math

import jax
import jax.numpy as jnp
from jax import lax
from jax.experimental import pallas as pl
from jax.experimental.pallas import tpu as pltpu
from jax.sharding import PartitionSpec as P

HD = 128
HOPS = 3
FAR = -1e30
AXES = ("ctx", "grp")
VMEM = pl.BlockSpec(memory_space=pltpu.VMEM)
HBM = pl.BlockSpec(memory_space=pltpu.HBM)
SCALE = math.log2(math.e) / math.sqrt(HD)
PARAMS = pltpu.CompilerParams(vmem_limit_bytes=40 * 2**20)


def shift_route(count, distance):
    return [(i, (i + distance) % count) for i in range(count)]


def flip_route(ctx_count, grp_count, flip):
    count = ctx_count * grp_count
    return [
        (i, (i + ((i % grp_count ^ flip) - i % grp_count) % grp_count) % count)
        for i in range(count)
    ]


def compose_route(wanted, first):
    holder = dict(first)
    return [(holder[s], d) for s, d in wanted]


def segments_at(len_ref, positions, starts_of):
    steps = len_ref.shape[1]
    unroll = math.gcd(steps, 16)

    def step(block, carry):
        start, segs, begins = carry
        for k in range(unroll):
            s = block * unroll + k
            reached = [start <= position for position in positions]
            segs = [jnp.where(r, s, seg) for r, seg in zip(reached, segs)]
            begins = [jnp.where(r, start, begin) for r, begin in zip(reached, begins)]
            start = start + len_ref[0, s]
        return start, segs, begins

    zero = jnp.int32(0)
    carry = (zero, [zero] * len(positions), [zero] * starts_of)
    _, segs, begins = lax.fori_loop(0, steps // unroll, step, carry)
    return segs, begins


def block_mask(shape, hop, from_a, from_b):
    key = lax.broadcasted_iota(jnp.int32, shape, 0) - hop * shape[0]
    query = lax.broadcasted_iota(jnp.int32, shape, 1)
    start = jnp.where(query >= from_b, from_b, from_a)
    return jnp.where((key >= start) & (key <= query), 0.0, FAR).astype(jnp.bfloat16)


def all_masks(kinds, t, size, place_ref):
    from_a, from_b = (place_ref[i][:1, :1] for i in (4, 5))
    grp_count = lax.axis_size("grp")
    ends = [jnp.broadcast_to(x, (t, t)) for x in (from_a, from_b)]
    blocks = [block_mask((t, t), hop_of(k, grp_count), *ends) for k in kinds]
    b = jnp.broadcast_to(from_b, (size, t))
    is_b = (lax.broadcasted_iota(jnp.int32, (size, t), 1) >= b) & (b > 0)
    blocks[-1:-1] = [
        jnp.where(is_b, x, y).astype(jnp.bfloat16) for x, y in ((FAR, 0.0), (0.0, FAR))
    ]
    return blocks


def hop_of(kind, grp_count):
    me = lax.axis_index("grp")
    if kind[0] == "shift":
        return kind[1]
    return (me - (me ^ kind[1])) & (grp_count - 1)


def plan_kernel(t, plane, *refs):
    len_hbm, task_hbm, slot_hbm, bank_hbm, kv_hbm = refs[:5]
    place_ref, k_ref, v_ref = refs[5:8]
    out_refs = refs[8:-5]
    len_ref, task_ref, slot_ref, bank_ref, sems = refs[-5:]
    pairs = (
        (len_hbm, len_ref),
        (task_hbm, task_ref),
        (slot_hbm, slot_ref),
        (bank_hbm, bank_ref),
        (kv_hbm.at[pl.ds(0, 1)], k_ref),
        (kv_hbm.at[pl.ds(1, 1)], v_ref),
    )
    copies = [pltpu.make_async_copy(x, y, sems.at[i]) for i, (x, y) in enumerate(pairs)]
    for copy in copies:
        copy.start()
    for copy in copies[:3]:
        copy.wait()
    grp_count = lax.axis_size("grp")
    me = lax.axis_index("grp")
    row_base = lax.axis_index("ctx") * grp_count
    held = bank_ref.shape[1]
    first = (row_base + me) * t
    positions = [first, first + (t - 1)]
    groups = []
    if plane:
        across = me ^ 2
        groups = [[me, me + 1], [me ^ 1, (me ^ 1) + 1], [(across & 2) + k for k in range(3)]]
        positions += [(row_base + k) * t for group in groups for k in group]
    segs, begins = segments_at(len_ref, positions, 2)
    for i, begin in enumerate(begins):
        place_ref[4 + i] = jnp.full(place_ref.shape[1:], begin - first, jnp.int32)
    if plane:
        rows = [slot_ref[task_ref[0, seg]] for seg in segs[2:]]
        for i, row in enumerate(rows[:4]):
            place_ref[i] = jnp.full(place_ref.shape[1:], (row // held) ^ me, jnp.int32)
        copies[3].wait()
        for group, out_ref in zip(groups, out_refs):
            for i in range(len(group)):
                local = jnp.clip(rows.pop(0) - me * held, 0, held - 1)
                for part in range(2):
                    out_ref[i, part] = bank_ref[part, local]
    for copy in copies[4 if plane else 3 :]:
        copy.wait()


def here(place_ref, i, place, shape):
    return jnp.broadcast_to(place_ref[i][:1, :1] == place, shape)


def pass_kernel(in_ref, out_ref):
    out_ref[...] = in_ref[...]


def relay_kernel(place_ref, mine_ref, got_ref, out_ref):
    at = (lax.axis_index("grp") ^ 1) & 1
    for slot in range(2):
        for part in range(2):
            got = got_ref[at + slot, part]
            own = here(place_ref, 2 + slot, 0, got.shape)
            out_ref[slot, part] = jnp.where(own, mine_ref[slot, part], got)


def eye(t):
    a, b = (lax.broadcasted_iota(jnp.int32, (t, t), i) for i in range(2))
    return (a == b).astype(jnp.float32).astype(jnp.bfloat16)


def staged(count, score, weigh, mix):
    scores, weights = {}, {}
    for i in range(count + 2):
        if i < count:
            scores[i] = score(i)
        if 0 <= i - 1 < count:
            weights[i - 1] = weigh(i - 1, scores.pop(i - 1))
        if 0 <= i - 2 < count:
            mix(i - 2, weights.pop(i - 2))


def score(keys, masks, q):
    t = masks.shape[1]
    ones = jnp.concatenate([eye(t)] * (q.shape[1] // t), axis=1)
    return jnp.dot(
        jnp.concatenate([keys, masks], axis=1),
        jnp.concatenate([q, ones], axis=0),
        preferred_element_type=jnp.float32,
    )


def mix(values, weights):
    v = jnp.concatenate([values.T, jnp.ones((16, values.shape[0]), jnp.bfloat16)], axis=0)
    return jnp.dot(v, weights, preferred_element_type=jnp.float32)


def lanes(j):
    return slice(j * HD, (j + 1) * HD)


def own_kernel(groups, kinds, size, place_ref, q_hbm, k_ref, v_ref, *refs):
    mask_ref, qt_ref, acc_ref, sum_ref, top_ref, q_ref, sem = refs
    copy = pltpu.make_async_copy(q_hbm, q_ref, sem)
    copy.start()
    t = q_ref.shape[1]
    blocks = all_masks(kinds, t, size, place_ref)
    mask_ref[...] = jnp.concatenate(blocks, axis=0)
    copy.wait()

    def scored(j):
        q = jnp.concatenate([q_ref[0, :, lanes(j * groups + g)].T for g in range(groups)], axis=1)
        qt_ref[j] = q
        return score(k_ref[0, 0, :, lanes(j)], blocks[0], q)

    def weighed(j, s):
        top = jnp.max(s, axis=0, keepdims=True) * SCALE
        top_ref[j : j + 1, :] = top
        return jnp.exp2(s * SCALE - top).astype(jnp.bfloat16)

    def mixed(j, w):
        o = mix(v_ref[0, 0, :, lanes(j)], w)
        acc_ref[j] = o[:HD]
        sum_ref[j : j + 1, :] = o[HD : HD + 1]

    staged(acc_ref.shape[0], scored, weighed, mixed)


def merge(rows, masks, qt_ref, old, finish):
    acc_ref, sum_ref, top_ref = old

    def scored(j):
        return score(rows(0, j), masks, qt_ref[j])

    def weighed(j, s):
        before = top_ref[j : j + 1, :]
        top = jnp.maximum(jnp.max(s, axis=0, keepdims=True) * SCALE, before)
        return jnp.exp2(s * SCALE - top).astype(jnp.bfloat16), jnp.exp2(before - top), top

    def mixed(j, step):
        w, keep, top = step
        o = mix(rows(1, j), w)
        finish(j, acc_ref[j], o[:HD], keep, sum_ref[j : j + 1, :] * keep + o[HD : HD + 1], top)

    staged(acc_ref.shape[0], scored, weighed, mixed)


def near_kernel(mask_ref, qt_ref, *refs):
    kv_refs, old, new = refs[:-6], refs[-6:-3], refs[-3:]
    acc_ref, sum_ref, top_ref = new
    t = mask_ref.shape[1]
    count = len(kv_refs) // 2

    def rows(part, j):
        return jnp.concatenate([r[0, 0, :, lanes(j)] for r in kv_refs[part::2]], axis=0)

    def finish(j, acc, more, keep, total, top):
        acc_ref[j] = acc * keep + more
        sum_ref[j : j + 1, :] = total
        top_ref[j : j + 1, :] = top

    merge(rows, mask_ref[t : (1 + count) * t, :], qt_ref, old, finish)


def far_kernel(groups, plane, kind, mask_ref, qt_ref, k_ref, v_ref, *refs):
    prefix_refs, old, (out_hbm, out_ref, sems) = refs[:-6], refs[-6:-3], refs[-3:]
    t = mask_ref.shape[1]
    size = prefix_refs[-1].shape[2]
    picked = [[], []]
    for part in range(2):
        for slot in range(2):
            value = prefix_refs[-1][slot, part]
            if plane:
                place_ref, own_ref, got_ref = prefix_refs[:3]
                got = got_ref[(lax.axis_index("grp") & 1) + slot, part]
                value = jnp.where(here(place_ref, slot, 2, value.shape), got, value)
                value = jnp.where(here(place_ref, slot, 0, value.shape), own_ref[slot, part], value)
            picked[part].append(value)

    def attend_to(with_block):
        copies = []

        def rows(part, j):
            parts = [p[:, lanes(j)] for p in picked[part]]
            if with_block:
                parts.append((k_ref, v_ref)[part][0, 0, :, lanes(j)])
            return jnp.concatenate(parts, axis=0)

        def finish(j, acc, more, keep, total, top):
            part = 1.0 / total
            done = acc * (keep * part) + more * part
            for g in range(groups):
                out_ref[0, :, lanes(j * groups + g)] = (
                    done[:, g * t : (g + 1) * t].T.astype(out_ref.dtype)
                )
            cols = pl.ds(j * groups * HD, groups * HD)
            copies.append(
                pltpu.make_async_copy(out_ref.at[:, :, cols], out_hbm.at[:, :, cols], sems.at[j])
            )
            copies[-1].start()

        start = mask_ref.shape[0] - t - 2 * size
        count = 2 * size + (t if with_block else 0)
        merge(rows, mask_ref[start : start + count, :], qt_ref, old, finish)
        for copy in copies:
            copy.wait()

    grp_count = lax.axis_size("grp")
    shard = lax.axis_index("ctx") * grp_count + lax.axis_index("grp")
    exists = shard >= hop_of(kind, grp_count)
    pl.when(exists)(functools.partial(attend_to, True))
    pl.when(jnp.logical_not(exists))(functools.partial(attend_to, False))


def on_device(queries, keyvals, seg_len, seg_task, task_slot, prefix_bank):
    ctx_count, grp_count = (lax.axis_size(a) for a in AXES)
    t = queries.shape[1]
    kv_heads = keyvals.shape[3] // HD
    groups = queries.shape[2] // keyvals.shape[3]
    plane = grp_count == HOPS + 1
    row_shape = (2,) + prefix_bank.shape[2:]
    if plane:
        kinds = [("shift", 0)] + [("flip", k) for k in range(1, HOPS + 1)]
        near, side, far = (flip_route(ctx_count, grp_count, k) for k in range(1, HOPS + 1))
    else:
        kinds = [("shift", d) for d in range(HOPS + 1)]
        near, side, far = (shift_route(ctx_count * grp_count, d) for d in range(1, HOPS + 1))

    def struct(shape, dtype):
        return jax.ShapeDtypeStruct(shape, dtype)

    def in_hbm(array):
        return pltpu.with_memory_space_constraint(array, pltpu.HBM)

    def rows_of(count):
        return struct((count,) + row_shape, prefix_bank.dtype)

    def flip(array, k):
        return lax.ppermute(array, "grp", [(i, i ^ k) for i in range(grp_count)])

    def cost(quarters):
        return pl.CostEstimate(
            flops=quarters * queries.size * t,
            bytes_accessed=quarters * queries.size // 2,
            transcendentals=quarters * queries.size // 4,
        )

    extra = [struct((4, 8, 128), jnp.int32)] + [rows_of(n) for n in (2, 2, 3)] if plane else []
    half = struct((1,) + keyvals.shape[1:], keyvals.dtype)
    arguments = (seg_len, seg_task, task_slot, prefix_bank, keyvals)
    outputs = [struct((6, 8, 128), jnp.int32), half, half]
    outputs += [rows_of(n) for n in (2, 2, 3)] if plane else []
    place, keys, values, *planned = pl.pallas_call(
        functools.partial(plan_kernel, t, plane),
        out_shape=outputs,
        in_specs=[HBM] * len(arguments),
        out_specs=[VMEM] * len(outputs),
        scratch_shapes=[pltpu.SMEM(a.shape, a.dtype) for a in arguments[:3]]
        + [pltpu.VMEM(prefix_bank.shape, prefix_bank.dtype), pltpu.SemaphoreType.DMA((6,))],
        compiler_params=PARAMS,
        name="plan",
    )(*(in_hbm(a) for a in arguments))

    side_keys = lax.ppermute(keys, AXES, side)
    near_values = lax.ppermute(values, AXES, near)
    if plane:
        own_rows, near_rows, side_rows = planned
        got_rows = flip(side_rows, 2)
    near_keys = lax.ppermute(keys, AXES, near)
    side_values = lax.ppermute(values, AXES, side)
    if plane:
        far_keys = lax.ppermute(side_keys, AXES, compose_route(far, side))
        far_values = lax.ppermute(near_values, AXES, compose_route(far, near))
        relayed = pl.pallas_call(
            relay_kernel,
            out_shape=rows_of(2),
            in_specs=[VMEM] * 3,
            out_specs=VMEM,
            compiler_params=PARAMS,
            cost_estimate=cost(32),
            name="relay_rows",
        )(place, near_rows, got_rows)
        relayed = pl.pallas_call(
            pass_kernel,
            out_shape=rows_of(2),
            in_specs=[VMEM],
            out_specs=VMEM,
            compiler_params=PARAMS,
            cost_estimate=cost(4),
            name="settle",
        )(flip(relayed, 1))
        prefix = [place, own_rows, got_rows, relayed]
    else:
        prefix = [fetch_prefix(seg_len, seg_task, task_slot, prefix_bank, t)]
        far_keys = lax.ppermute(keys, AXES, far)
        far_values = lax.ppermute(values, AXES, far)

    wide = struct((kv_heads, HD, groups * t), jnp.float32)
    flat = struct((kv_heads, groups * t), jnp.float32)
    masks, turned, *state = pl.pallas_call(
        functools.partial(own_kernel, groups, kinds, row_shape[1]),
        out_shape=[
            struct((len(kinds) * t + 2 * row_shape[1], t), jnp.bfloat16),
            struct(wide.shape, queries.dtype),
            wide,
            flat,
            flat,
        ],
        in_specs=[VMEM, HBM, VMEM, VMEM],
        out_specs=[VMEM] * 5,
        scratch_shapes=[pltpu.VMEM(queries.shape, queries.dtype), pltpu.SemaphoreType.DMA],
        compiler_params=PARAMS,
        cost_estimate=cost(8),
        name="attend_own",
    )(place, in_hbm(queries), keys, values)
    state = pl.pallas_call(
        near_kernel,
        out_shape=[wide, flat, flat],
        in_specs=[VMEM] * 9,
        out_specs=[VMEM] * 3,
        compiler_params=PARAMS,
        cost_estimate=cost(2),
        name="attend_near",
    )(masks, turned, near_keys, near_values, side_keys, side_values, *state)
    return pl.pallas_call(
        functools.partial(far_kernel, groups, plane, kinds[-1]),
        out_shape=struct(queries.shape, queries.dtype),
        in_specs=[VMEM] * (7 + len(prefix)),
        out_specs=HBM,
        scratch_shapes=[
            pltpu.VMEM(queries.shape, queries.dtype),
            pltpu.SemaphoreType.DMA((kv_heads,)),
        ],
        compiler_params=PARAMS,
        cost_estimate=cost(4),
        name="attend_far",
    )(masks, turned, far_keys, far_values, *prefix, *state)


def fetch_prefix(seg_len, seg_task, task_slot, prefix_bank, t):
    grp_count = lax.axis_size("grp")
    me = lax.axis_index("grp")
    held = prefix_bank.shape[1]
    starts = jnp.cumsum(seg_len[0]) - seg_len[0]
    shards = lax.axis_index("ctx") * grp_count + jnp.arange(grp_count, dtype=jnp.int32)
    ends = shards[:, None] * t + jnp.array([0, t - 1], jnp.int32)
    segs = jnp.sum((starts[None, None, :] <= ends[:, :, None]).astype(jnp.int32), axis=2) - 1
    rows = task_slot[seg_task[0][segs]]
    local = jnp.clip(rows - me * held, 0, held - 1)
    pieces = jnp.swapaxes(prefix_bank, 0, 1)[local]
    got = lax.all_to_all(pieces, "grp", split_axis=0, concat_axis=0, tiled=True)
    owner = rows[me] // held
    return jnp.stack([got[owner[s], s] for s in range(2)])


def solution(mesh):
    in_specs = (
        P(None, AXES, None),
        P(None, None, AXES, None),
        P(),
        P(),
        P(),
        P(None, "grp", None, None),
    )
    return jax.shard_map(
        on_device, mesh=mesh, in_specs=in_specs, out_specs=P(None, AXES, None), check_vma=False
    )
```

```python
import functools
import math

import jax
import jax.numpy as jnp
from jax import lax
from jax.experimental import pallas as pl
from jax.experimental.pallas import tpu as pltpu
from jax.sharding import PartitionSpec as P

HD = 128
HOPS = 3
FAR = -1e30
AXES = ("ctx", "grp")
VMEM = pl.BlockSpec(memory_space=pltpu.VMEM)
HBM = pl.BlockSpec(memory_space=pltpu.HBM)
SCALE = math.log2(math.e) / math.sqrt(HD)
PARAMS = pltpu.CompilerParams(vmem_limit_bytes=40 * 2**20)


def shift_route(count, distance):
    return [(i, (i + distance) % count) for i in range(count)]


def flip_route(ctx_count, grp_count, flip):
    count = ctx_count * grp_count
    return [
        (i, (i + ((i % grp_count ^ flip) - i % grp_count) % grp_count) % count)
        for i in range(count)
    ]


def compose_route(wanted, first):
    holder = dict(first)
    return [(holder[s], d) for s, d in wanted]


def segments_at(len_ref, positions, starts_of):
    steps = len_ref.shape[1]
    unroll = math.gcd(steps, 16)

    def step(block, carry):
        start, segs, begins = carry
        for k in range(unroll):
            s = block * unroll + k
            reached = [start <= position for position in positions]
            segs = [jnp.where(r, s, seg) for r, seg in zip(reached, segs)]
            begins = [jnp.where(r, start, begin) for r, begin in zip(reached, begins)]
            start = start + len_ref[0, s]
        return start, segs, begins

    zero = jnp.int32(0)
    carry = (zero, [zero] * len(positions), [zero] * starts_of)
    _, segs, begins = lax.fori_loop(0, steps // unroll, step, carry)
    return segs, begins


def block_mask(shape, hop, from_a, from_b):
    key = lax.broadcasted_iota(jnp.int32, shape, 0) - hop * shape[0]
    query = lax.broadcasted_iota(jnp.int32, shape, 1)
    start = jnp.where(query >= from_b, from_b, from_a)
    return jnp.where((key >= start) & (key <= query), 0.0, FAR).astype(jnp.bfloat16)


def all_masks(kinds, t, size, place_ref):
    from_a, from_b = (place_ref[i][:1, :1] for i in (4, 5))
    grp_count = lax.axis_size("grp")
    ends = [jnp.broadcast_to(x, (t, t)) for x in (from_a, from_b)]
    blocks = [block_mask((t, t), hop_of(k, grp_count), *ends) for k in kinds]
    b = jnp.broadcast_to(from_b, (size, t))
    is_b = (lax.broadcasted_iota(jnp.int32, (size, t), 1) >= b) & (b > 0)
    blocks[-1:-1] = [
        jnp.where(is_b, x, y).astype(jnp.bfloat16) for x, y in ((FAR, 0.0), (0.0, FAR))
    ]
    return blocks


def hop_of(kind, grp_count):
    me = lax.axis_index("grp")
    if kind[0] == "shift":
        return kind[1]
    return (me - (me ^ kind[1])) & (grp_count - 1)


def plan_kernel(t, plane, *refs):
    len_hbm, task_hbm, slot_hbm, bank_hbm, kv_hbm = refs[:5]
    place_ref, k_ref, v_ref = refs[5:8]
    out_refs = refs[8:-5]
    len_ref, task_ref, slot_ref, bank_ref, sems = refs[-5:]
    pairs = (
        (len_hbm, len_ref),
        (task_hbm, task_ref),
        (slot_hbm, slot_ref),
        (bank_hbm, bank_ref),
        (kv_hbm.at[pl.ds(0, 1)], k_ref),
        (kv_hbm.at[pl.ds(1, 1)], v_ref),
    )
    copies = [pltpu.make_async_copy(x, y, sems.at[i]) for i, (x, y) in enumerate(pairs)]
    for copy in copies:
        copy.start()
    for copy in copies[:3]:
        copy.wait()
    grp_count = lax.axis_size("grp")
    me = lax.axis_index("grp")
    row_base = lax.axis_index("ctx") * grp_count
    held = bank_ref.shape[1]
    first = (row_base + me) * t
    positions = [first, first + (t - 1)]
    groups = []
    if plane:
        across = me ^ 2
        groups = [[me, me + 1], [me ^ 1, (me ^ 1) + 1], [(across & 2) + k for k in range(3)]]
        positions += [(row_base + k) * t for group in groups for k in group]
    segs, begins = segments_at(len_ref, positions, 2)
    for i, begin in enumerate(begins):
        place_ref[4 + i] = jnp.full(place_ref.shape[1:], begin - first, jnp.int32)
    if plane:
        rows = [slot_ref[task_ref[0, seg]] for seg in segs[2:]]
        for i, row in enumerate(rows[:4]):
            place_ref[i] = jnp.full(place_ref.shape[1:], (row // held) ^ me, jnp.int32)
        copies[3].wait()
        for group, out_ref in zip(groups, out_refs):
            for i in range(len(group)):
                local = jnp.clip(rows.pop(0) - me * held, 0, held - 1)
                for part in range(2):
                    out_ref[i, part] = bank_ref[part, local]
    for copy in copies[4 if plane else 3 :]:
        copy.wait()


def here(place_ref, i, place, shape):
    return jnp.broadcast_to(place_ref[i][:1, :1] == place, shape)


def pass_kernel(in_ref, out_ref):
    out_ref[...] = in_ref[...]


def relay_kernel(place_ref, mine_ref, got_ref, out_ref):
    at = (lax.axis_index("grp") ^ 1) & 1
    for slot in range(2):
        for part in range(2):
            got = got_ref[at + slot, part]
            own = here(place_ref, 2 + slot, 0, got.shape)
            out_ref[slot, part] = jnp.where(own, mine_ref[slot, part], got)


def eye(t):
    a, b = (lax.broadcasted_iota(jnp.int32, (t, t), i) for i in range(2))
    return (a == b).astype(jnp.float32).astype(jnp.bfloat16)


def staged(count, score, weigh, mix):
    scores, weights = {}, {}
    for i in range(count + 2):
        if i < count:
            scores[i] = score(i)
        if 0 <= i - 1 < count:
            weights[i - 1] = weigh(i - 1, scores.pop(i - 1))
        if 0 <= i - 2 < count:
            mix(i - 2, weights.pop(i - 2))


def score(keys, masks, q):
    t = masks.shape[1]
    groups = q.shape[1] // t
    if keys.shape[0] < t:
        s = jnp.dot(keys, q, preferred_element_type=jnp.float32)
        return s + jnp.concatenate([masks.astype(jnp.float32)] * groups, axis=1)
    ones = jnp.concatenate([eye(t)] * groups, axis=1)
    return jnp.dot(
        jnp.concatenate([keys, masks], axis=1),
        jnp.concatenate([q, ones], axis=0),
        preferred_element_type=jnp.float32,
    )


def mix(values, weights):
    v = jnp.concatenate([values.T, jnp.ones((16, values.shape[0]), jnp.bfloat16)], axis=0)
    return jnp.dot(v, weights, preferred_element_type=jnp.float32)


def lanes(j):
    return slice(j * HD, (j + 1) * HD)


def own_kernel(groups, kinds, size, place_ref, q_hbm, k_ref, v_ref, *refs):
    mask_ref, qt_ref, acc_ref, sum_ref, top_ref, q_ref, sem = refs
    copy = pltpu.make_async_copy(q_hbm, q_ref, sem)
    copy.start()
    t = q_ref.shape[1]
    blocks = all_masks(kinds, t, size, place_ref)
    mask_ref[...] = jnp.concatenate(blocks, axis=0)
    copy.wait()

    def scored(j):
        q = jnp.concatenate([q_ref[0, :, lanes(j * groups + g)].T for g in range(groups)], axis=1)
        qt_ref[j] = q
        return score(k_ref[0, 0, :, lanes(j)], blocks[0], q)

    def weighed(j, s):
        top = jnp.max(s, axis=0, keepdims=True) * SCALE
        top_ref[j : j + 1, :] = top
        return jnp.exp2(s * SCALE - top).astype(jnp.bfloat16)

    def mixed(j, w):
        o = mix(v_ref[0, 0, :, lanes(j)], w)
        acc_ref[j] = o[:HD]
        sum_ref[j : j + 1, :] = o[HD : HD + 1]

    staged(acc_ref.shape[0], scored, weighed, mixed)


def merge(rows, masks, qt_ref, old, finish):
    acc_ref, sum_ref, top_ref = old

    def scored(j):
        return score(rows(0, j), masks, qt_ref[j])

    def weighed(j, s):
        before = top_ref[j : j + 1, :]
        top = jnp.maximum(jnp.max(s, axis=0, keepdims=True) * SCALE, before)
        return jnp.exp2(s * SCALE - top).astype(jnp.bfloat16), jnp.exp2(before - top), top

    def mixed(j, step):
        w, keep, top = step
        o = mix(rows(1, j), w)
        finish(j, acc_ref[j], o[:HD], keep, sum_ref[j : j + 1, :] * keep + o[HD : HD + 1], top)

    staged(acc_ref.shape[0], scored, weighed, mixed)


def near_kernel(mask_ref, qt_ref, *refs):
    kv_refs, old, new = refs[:-6], refs[-6:-3], refs[-3:]
    acc_ref, sum_ref, top_ref = new
    t = mask_ref.shape[1]
    count = len(kv_refs) // 2

    def rows(part, j):
        return jnp.concatenate([r[0, 0, :, lanes(j)] for r in kv_refs[part::2]], axis=0)

    def finish(j, acc, more, keep, total, top):
        acc_ref[j] = acc * keep + more
        sum_ref[j : j + 1, :] = total
        top_ref[j : j + 1, :] = top

    merge(rows, mask_ref[t : (1 + count) * t, :], qt_ref, old, finish)


def far_kernel(groups, plane, kind, mask_ref, qt_ref, k_ref, v_ref, *refs):
    prefix_refs, old, (out_hbm, out_ref, sems) = refs[:-6], refs[-6:-3], refs[-3:]
    t = mask_ref.shape[1]
    size = prefix_refs[-1].shape[2]
    picked = [[], []]
    for part in range(2):
        for slot in range(2):
            value = prefix_refs[-1][slot, part]
            if plane:
                place_ref, own_ref, got_ref = prefix_refs[:3]
                got = got_ref[(lax.axis_index("grp") & 1) + slot, part]
                value = jnp.where(here(place_ref, slot, 2, value.shape), got, value)
                value = jnp.where(here(place_ref, slot, 0, value.shape), own_ref[slot, part], value)
            picked[part].append(value)

    def attend_to(with_block):
        copies = []

        def rows(part, j):
            parts = [p[:, lanes(j)] for p in picked[part]]
            if with_block:
                parts.append((k_ref, v_ref)[part][0, 0, :, lanes(j)])
            return jnp.concatenate(parts, axis=0)

        def finish(j, acc, more, keep, total, top):
            part = 1.0 / total
            done = acc * (keep * part) + more * part
            for g in range(groups):
                out_ref[0, :, lanes(j * groups + g)] = (
                    done[:, g * t : (g + 1) * t].T.astype(out_ref.dtype)
                )
            cols = pl.ds(j * groups * HD, groups * HD)
            copies.append(
                pltpu.make_async_copy(out_ref.at[:, :, cols], out_hbm.at[:, :, cols], sems.at[j])
            )
            copies[-1].start()

        start = mask_ref.shape[0] - t - 2 * size
        count = 2 * size + (t if with_block else 0)
        merge(rows, mask_ref[start : start + count, :], qt_ref, old, finish)
        for copy in copies:
            copy.wait()

    grp_count = lax.axis_size("grp")
    shard = lax.axis_index("ctx") * grp_count + lax.axis_index("grp")
    exists = shard >= hop_of(kind, grp_count)
    pl.when(exists)(functools.partial(attend_to, True))
    pl.when(jnp.logical_not(exists))(functools.partial(attend_to, False))


def on_device(queries, keyvals, seg_len, seg_task, task_slot, prefix_bank):
    ctx_count, grp_count = (lax.axis_size(a) for a in AXES)
    t = queries.shape[1]
    kv_heads = keyvals.shape[3] // HD
    groups = queries.shape[2] // keyvals.shape[3]
    plane = grp_count == HOPS + 1
    row_shape = (2,) + prefix_bank.shape[2:]
    if plane:
        kinds = [("shift", 0)] + [("flip", k) for k in range(1, HOPS + 1)]
        near, side, far = (flip_route(ctx_count, grp_count, k) for k in range(1, HOPS + 1))
    else:
        kinds = [("shift", d) for d in range(HOPS + 1)]
        near, side, far = (shift_route(ctx_count * grp_count, d) for d in range(1, HOPS + 1))

    def struct(shape, dtype):
        return jax.ShapeDtypeStruct(shape, dtype)

    def in_hbm(array):
        return pltpu.with_memory_space_constraint(array, pltpu.HBM)

    def rows_of(count):
        return struct((count,) + row_shape, prefix_bank.dtype)

    def flip(array, k):
        return lax.ppermute(array, "grp", [(i, i ^ k) for i in range(grp_count)])

    def cost(quarters):
        return pl.CostEstimate(
            flops=quarters * queries.size * t,
            bytes_accessed=quarters * queries.size // 2,
            transcendentals=quarters * queries.size // 4,
        )

    extra = [struct((4, 8, 128), jnp.int32)] + [rows_of(n) for n in (2, 2, 3)] if plane else []
    half = struct((1,) + keyvals.shape[1:], keyvals.dtype)
    arguments = (seg_len, seg_task, task_slot, prefix_bank, keyvals)
    outputs = [struct((6, 8, 128), jnp.int32), half, half]
    outputs += [rows_of(n) for n in (2, 2, 3)] if plane else []
    place, keys, values, *planned = pl.pallas_call(
        functools.partial(plan_kernel, t, plane),
        out_shape=outputs,
        in_specs=[HBM] * len(arguments),
        out_specs=[VMEM] * len(outputs),
        scratch_shapes=[pltpu.SMEM(a.shape, a.dtype) for a in arguments[:3]]
        + [pltpu.VMEM(prefix_bank.shape, prefix_bank.dtype), pltpu.SemaphoreType.DMA((6,))],
        compiler_params=PARAMS,
        name="plan",
    )(*(in_hbm(a) for a in arguments))

    side_keys = lax.ppermute(keys, AXES, side)
    near_values = lax.ppermute(values, AXES, near)
    if plane:
        own_rows, near_rows, side_rows = planned
        got_rows = flip(side_rows, 2)
    near_keys = lax.ppermute(keys, AXES, near)
    side_values = lax.ppermute(values, AXES, side)
    if plane:
        far_keys = lax.ppermute(side_keys, AXES, compose_route(far, side))
        far_values = lax.ppermute(near_values, AXES, compose_route(far, near))
        relayed = pl.pallas_call(
            relay_kernel,
            out_shape=rows_of(2),
            in_specs=[VMEM] * 3,
            out_specs=VMEM,
            compiler_params=PARAMS,
            cost_estimate=cost(32),
            name="relay_rows",
        )(place, near_rows, got_rows)
        relayed = pl.pallas_call(
            pass_kernel,
            out_shape=rows_of(2),
            in_specs=[VMEM],
            out_specs=VMEM,
            compiler_params=PARAMS,
            cost_estimate=cost(4),
            name="settle",
        )(flip(relayed, 1))
        prefix = [place, own_rows, got_rows, relayed]
    else:
        prefix = [fetch_prefix(seg_len, seg_task, task_slot, prefix_bank, t)]
        far_keys = lax.ppermute(keys, AXES, far)
        far_values = lax.ppermute(values, AXES, far)

    wide = struct((kv_heads, HD, groups * t), jnp.float32)
    flat = struct((kv_heads, groups * t), jnp.float32)
    masks, turned, *state = pl.pallas_call(
        functools.partial(own_kernel, groups, kinds, row_shape[1]),
        out_shape=[
            struct((len(kinds) * t + 2 * row_shape[1], t), jnp.bfloat16),
            struct(wide.shape, queries.dtype),
            wide,
            flat,
            flat,
        ],
        in_specs=[VMEM, HBM, VMEM, VMEM],
        out_specs=[VMEM] * 5,
        scratch_shapes=[pltpu.VMEM(queries.shape, queries.dtype), pltpu.SemaphoreType.DMA],
        compiler_params=PARAMS,
        cost_estimate=cost(8),
        name="attend_own",
    )(place, in_hbm(queries), keys, values)
    state = pl.pallas_call(
        near_kernel,
        out_shape=[wide, flat, flat],
        in_specs=[VMEM] * 9,
        out_specs=[VMEM] * 3,
        compiler_params=PARAMS,
        cost_estimate=cost(2),
        name="attend_near",
    )(masks, turned, near_keys, near_values, side_keys, side_values, *state)
    return pl.pallas_call(
        functools.partial(far_kernel, groups, plane, kinds[-1]),
        out_shape=struct(queries.shape, queries.dtype),
        in_specs=[VMEM] * (7 + len(prefix)),
        out_specs=HBM,
        scratch_shapes=[
            pltpu.VMEM(queries.shape, queries.dtype),
            pltpu.SemaphoreType.DMA((kv_heads,)),
        ],
        compiler_params=PARAMS,
        cost_estimate=cost(4),
        name="attend_far",
    )(masks, turned, far_keys, far_values, *prefix, *state)


def fetch_prefix(seg_len, seg_task, task_slot, prefix_bank, t):
    grp_count = lax.axis_size("grp")
    me = lax.axis_index("grp")
    held = prefix_bank.shape[1]
    starts = jnp.cumsum(seg_len[0]) - seg_len[0]
    shards = lax.axis_index("ctx") * grp_count + jnp.arange(grp_count, dtype=jnp.int32)
    ends = shards[:, None] * t + jnp.array([0, t - 1], jnp.int32)
    segs = jnp.sum((starts[None, None, :] <= ends[:, :, None]).astype(jnp.int32), axis=2) - 1
    rows = task_slot[seg_task[0][segs]]
    local = jnp.clip(rows - me * held, 0, held - 1)
    pieces = jnp.swapaxes(prefix_bank, 0, 1)[local]
    got = lax.all_to_all(pieces, "grp", split_axis=0, concat_axis=0, tiled=True)
    owner = rows[me] // held
    return jnp.stack([got[owner[s], s] for s in range(2)])


def solution(mesh):
    in_specs = (
        P(None, AXES, None),
        P(None, None, AXES, None),
        P(),
        P(),
        P(),
        P(None, "grp", None, None),
    )
    return jax.shard_map(
        on_device, mesh=mesh, in_specs=in_specs, out_specs=P(None, AXES, None), check_vma=False
    )
```

```python
import functools
import math

import jax
import jax.numpy as jnp
from jax import lax
from jax.experimental import pallas as pl
from jax.experimental.pallas import tpu as pltpu
from jax.sharding import PartitionSpec as P

HD = 128
HOPS = 3
FAR = -1e30
AXES = ("ctx", "grp")
VMEM = pl.BlockSpec(memory_space=pltpu.VMEM)
HBM = pl.BlockSpec(memory_space=pltpu.HBM)
SCALE = math.log2(math.e) / math.sqrt(HD)
PARAMS = pltpu.CompilerParams(vmem_limit_bytes=40 * 2**20)


def shift_route(count, distance):
    return [(i, (i + distance) % count) for i in range(count)]


def flip_route(ctx_count, grp_count, flip):
    count = ctx_count * grp_count
    return [
        (i, (i + ((i % grp_count ^ flip) - i % grp_count) % grp_count) % count)
        for i in range(count)
    ]


def compose_route(wanted, first):
    holder = dict(first)
    return [(holder[s], d) for s, d in wanted]


def segments_at(len_ref, positions, starts_of):
    steps = len_ref.shape[1]
    unroll = math.gcd(steps, 16)

    def step(block, carry):
        start, segs, begins = carry
        for k in range(unroll):
            s = block * unroll + k
            reached = [start <= position for position in positions]
            segs = [jnp.where(r, s, seg) for r, seg in zip(reached, segs)]
            begins = [jnp.where(r, start, begin) for r, begin in zip(reached, begins)]
            start = start + len_ref[0, s]
        return start, segs, begins

    zero = jnp.int32(0)
    carry = (zero, [zero] * len(positions), [zero] * starts_of)
    _, segs, begins = lax.fori_loop(0, steps // unroll, step, carry)
    return segs, begins


def block_mask(shape, hop, from_a, from_b):
    key = lax.broadcasted_iota(jnp.int32, shape, 0) - hop * shape[0]
    query = lax.broadcasted_iota(jnp.int32, shape, 1)
    start = jnp.where(query >= from_b, from_b, from_a)
    return jnp.where((key >= start) & (key <= query), 0.0, FAR).astype(jnp.bfloat16)


def all_masks(kinds, t, size, place_ref):
    from_a, from_b = (place_ref[i][:1, :1] for i in (4, 5))
    grp_count = lax.axis_size("grp")
    ends = [jnp.broadcast_to(x, (t, t)) for x in (from_a, from_b)]
    blocks = [block_mask((t, t), hop_of(k, grp_count), *ends) for k in kinds]
    b = jnp.broadcast_to(from_b, (size, t))
    is_b = (lax.broadcasted_iota(jnp.int32, (size, t), 1) >= b) & (b > 0)
    blocks[-1:-1] = [
        jnp.where(is_b, x, y).astype(jnp.bfloat16) for x, y in ((FAR, 0.0), (0.0, FAR))
    ]
    return blocks


def hop_of(kind, grp_count):
    me = lax.axis_index("grp")
    if kind[0] == "shift":
        return kind[1]
    return (me - (me ^ kind[1])) & (grp_count - 1)


def plan_kernel(t, plane, *refs):
    len_hbm, task_hbm, slot_hbm, bank_hbm, kv_hbm = refs[:5]
    place_ref, k_ref, v_ref = refs[5:8]
    out_refs = refs[8:-5]
    len_ref, task_ref, slot_ref, bank_ref, sems = refs[-5:]
    pairs = (
        (len_hbm, len_ref),
        (task_hbm, task_ref),
        (slot_hbm, slot_ref),
        (bank_hbm, bank_ref),
        (kv_hbm.at[pl.ds(0, 1)], k_ref),
        (kv_hbm.at[pl.ds(1, 1)], v_ref),
    )
    copies = [pltpu.make_async_copy(x, y, sems.at[i]) for i, (x, y) in enumerate(pairs)]
    for copy in copies:
        copy.start()
    for copy in copies[:3]:
        copy.wait()
    grp_count = lax.axis_size("grp")
    me = lax.axis_index("grp")
    row_base = lax.axis_index("ctx") * grp_count
    held = bank_ref.shape[1]
    first = (row_base + me) * t
    positions = [first, first + (t - 1)]
    groups = []
    if plane:
        across = me ^ 2
        groups = [[me, me + 1], [me ^ 1, (me ^ 1) + 1], [(across & 2) + k for k in range(3)]]
        positions += [(row_base + k) * t for group in groups for k in group]
    segs, begins = segments_at(len_ref, positions, 2)
    for i, begin in enumerate(begins):
        place_ref[4 + i] = jnp.full(place_ref.shape[1:], begin - first, jnp.int32)
    if plane:
        rows = [slot_ref[task_ref[0, seg]] for seg in segs[2:]]
        for i, row in enumerate(rows[:4]):
            place_ref[i] = jnp.full(place_ref.shape[1:], (row // held) ^ me, jnp.int32)
        copies[3].wait()
        for group, out_ref in zip(groups, out_refs):
            for i in range(len(group)):
                local = jnp.clip(rows.pop(0) - me * held, 0, held - 1)
                for part in range(2):
                    out_ref[i, part] = bank_ref[part, local]
    for copy in copies[4 if plane else 3 :]:
        copy.wait()


def here(place_ref, i, place, shape):
    return jnp.broadcast_to(place_ref[i][:1, :1] == place, shape)


def relay_kernel(place_ref, mine_ref, got_ref, out_ref):
    at = (lax.axis_index("grp") ^ 1) & 1
    for slot in range(2):
        for part in range(2):
            got = got_ref[at + slot, part]
            own = here(place_ref, 2 + slot, 0, got.shape)
            out_ref[slot, part] = jnp.where(own, mine_ref[slot, part], got)


def eye(t):
    a, b = (lax.broadcasted_iota(jnp.int32, (t, t), i) for i in range(2))
    return (a == b).astype(jnp.float32).astype(jnp.bfloat16)


def staged(count, score, weigh, mix):
    scores, weights = {}, {}
    for i in range(count + 2):
        if i < count:
            scores[i] = score(i)
        if 0 <= i - 1 < count:
            weights[i - 1] = weigh(i - 1, scores.pop(i - 1))
        if 0 <= i - 2 < count:
            mix(i - 2, weights.pop(i - 2))


def score(keys, masks, q):
    t = masks.shape[1]
    groups = q.shape[1] // t
    if keys.shape[0] < t:
        s = jnp.dot(keys, q, preferred_element_type=jnp.float32)
        return s + jnp.concatenate([masks.astype(jnp.float32)] * groups, axis=1)
    ones = jnp.concatenate([eye(t)] * groups, axis=1)
    return jnp.dot(
        jnp.concatenate([keys, masks], axis=1),
        jnp.concatenate([q, ones], axis=0),
        preferred_element_type=jnp.float32,
    )


def mix(values, weights):
    v = jnp.concatenate([values.T, jnp.ones((16, values.shape[0]), jnp.bfloat16)], axis=0)
    return jnp.dot(v, weights, preferred_element_type=jnp.float32)


def lanes(j):
    return slice(j * HD, (j + 1) * HD)


def own_kernel(groups, kinds, size, place_ref, q_hbm, k_ref, v_ref, *refs):
    mask_ref, qt_ref, acc_ref, sum_ref, top_ref, q_ref, sem = refs
    copy = pltpu.make_async_copy(q_hbm, q_ref, sem)
    copy.start()
    t = q_ref.shape[1]
    blocks = all_masks(kinds, t, size, place_ref)
    mask_ref[...] = jnp.concatenate(blocks, axis=0)
    copy.wait()

    def scored(j):
        q = jnp.concatenate([q_ref[0, :, lanes(j * groups + g)].T for g in range(groups)], axis=1)
        qt_ref[j] = q
        return score(k_ref[0, 0, :, lanes(j)], blocks[0], q)

    def weighed(j, s):
        top = jnp.max(s, axis=0, keepdims=True) * SCALE
        top_ref[j : j + 1, :] = top
        return jnp.exp2(s * SCALE - top).astype(jnp.bfloat16)

    def mixed(j, w):
        o = mix(v_ref[0, 0, :, lanes(j)], w)
        acc_ref[j] = o[:HD]
        sum_ref[j : j + 1, :] = o[HD : HD + 1]

    staged(acc_ref.shape[0], scored, weighed, mixed)


def merge(rows, masks, qt_ref, old, finish):
    acc_ref, sum_ref, top_ref = old

    def scored(j):
        return score(rows(0, j), masks, qt_ref[j])

    def weighed(j, s):
        before = top_ref[j : j + 1, :]
        top = jnp.maximum(jnp.max(s, axis=0, keepdims=True) * SCALE, before)
        return jnp.exp2(s * SCALE - top).astype(jnp.bfloat16), jnp.exp2(before - top), top

    def mixed(j, step):
        w, keep, top = step
        o = mix(rows(1, j), w)
        finish(j, acc_ref[j], o[:HD], keep, sum_ref[j : j + 1, :] * keep + o[HD : HD + 1], top)

    staged(acc_ref.shape[0], scored, weighed, mixed)


def near_kernel(mask_ref, qt_ref, *refs):
    kv_refs, old, new = refs[:-6], refs[-6:-3], refs[-3:]
    acc_ref, sum_ref, top_ref = new
    t = mask_ref.shape[1]
    count = len(kv_refs) // 2

    def rows(part, j):
        return jnp.concatenate([r[0, 0, :, lanes(j)] for r in kv_refs[part::2]], axis=0)

    def finish(j, acc, more, keep, total, top):
        acc_ref[j] = acc * keep + more
        sum_ref[j : j + 1, :] = total
        top_ref[j : j + 1, :] = top

    merge(rows, mask_ref[t : (1 + count) * t, :], qt_ref, old, finish)


def far_kernel(groups, plane, kind, mask_ref, qt_ref, k_ref, v_ref, *refs):
    prefix_refs, old, (out_hbm, out_ref, sems) = refs[:-6], refs[-6:-3], refs[-3:]
    t = mask_ref.shape[1]
    size = prefix_refs[-1].shape[2]
    picked = [[], []]
    for part in range(2):
        for slot in range(2):
            value = prefix_refs[-1][slot, part]
            if plane:
                place_ref, own_ref, got_ref = prefix_refs[:3]
                got = got_ref[(lax.axis_index("grp") & 1) + slot, part]
                value = jnp.where(here(place_ref, slot, 2, value.shape), got, value)
                value = jnp.where(here(place_ref, slot, 0, value.shape), own_ref[slot, part], value)
            picked[part].append(value)

    def attend_to(with_block):
        copies = []

        def rows(part, j):
            parts = [p[:, lanes(j)] for p in picked[part]]
            if with_block:
                parts.append((k_ref, v_ref)[part][0, 0, :, lanes(j)])
            return jnp.concatenate(parts, axis=0)

        def finish(j, acc, more, keep, total, top):
            part = 1.0 / total
            done = acc * (keep * part) + more * part
            for g in range(groups):
                out_ref[0, :, lanes(j * groups + g)] = (
                    done[:, g * t : (g + 1) * t].T.astype(out_ref.dtype)
                )
            cols = pl.ds(j * groups * HD, groups * HD)
            copies.append(
                pltpu.make_async_copy(out_ref.at[:, :, cols], out_hbm.at[:, :, cols], sems.at[j])
            )
            copies[-1].start()

        start = mask_ref.shape[0] - t - 2 * size
        count = 2 * size + (t if with_block else 0)
        merge(rows, mask_ref[start : start + count, :], qt_ref, old, finish)
        for copy in copies:
            copy.wait()

    grp_count = lax.axis_size("grp")
    shard = lax.axis_index("ctx") * grp_count + lax.axis_index("grp")
    exists = shard >= hop_of(kind, grp_count)
    pl.when(exists)(functools.partial(attend_to, True))
    pl.when(jnp.logical_not(exists))(functools.partial(attend_to, False))


def on_device(queries, keyvals, seg_len, seg_task, task_slot, prefix_bank):
    ctx_count, grp_count = (lax.axis_size(a) for a in AXES)
    t = queries.shape[1]
    kv_heads = keyvals.shape[3] // HD
    groups = queries.shape[2] // keyvals.shape[3]
    plane = grp_count == HOPS + 1
    row_shape = (2,) + prefix_bank.shape[2:]
    if plane:
        kinds = [("shift", 0)] + [("flip", k) for k in range(1, HOPS + 1)]
        near, side, far = (flip_route(ctx_count, grp_count, k) for k in range(1, HOPS + 1))
    else:
        kinds = [("shift", d) for d in range(HOPS + 1)]
        near, side, far = (shift_route(ctx_count * grp_count, d) for d in range(1, HOPS + 1))

    def struct(shape, dtype):
        return jax.ShapeDtypeStruct(shape, dtype)

    def in_hbm(array):
        return pltpu.with_memory_space_constraint(array, pltpu.HBM)

    def rows_of(count):
        return struct((count,) + row_shape, prefix_bank.dtype)

    def flip(array, k):
        return lax.ppermute(array, "grp", [(i, i ^ k) for i in range(grp_count)])

    def cost(quarters):
        return pl.CostEstimate(
            flops=quarters * queries.size * t,
            bytes_accessed=quarters * queries.size // 2,
            transcendentals=quarters * queries.size // 4,
        )

    extra = [struct((4, 8, 128), jnp.int32)] + [rows_of(n) for n in (2, 2, 3)] if plane else []
    half = struct((1,) + keyvals.shape[1:], keyvals.dtype)
    arguments = (seg_len, seg_task, task_slot, prefix_bank, keyvals)
    outputs = [struct((6, 8, 128), jnp.int32), half, half]
    outputs += [rows_of(n) for n in (2, 2, 3)] if plane else []
    place, keys, values, *planned = pl.pallas_call(
        functools.partial(plan_kernel, t, plane),
        out_shape=outputs,
        in_specs=[HBM] * len(arguments),
        out_specs=[VMEM] * len(outputs),
        scratch_shapes=[pltpu.SMEM(a.shape, a.dtype) for a in arguments[:3]]
        + [pltpu.VMEM(prefix_bank.shape, prefix_bank.dtype), pltpu.SemaphoreType.DMA((6,))],
        compiler_params=PARAMS,
        name="plan",
    )(*(in_hbm(a) for a in arguments))

    side_keys = lax.ppermute(keys, AXES, side)
    near_values = lax.ppermute(values, AXES, near)
    if plane:
        own_rows, near_rows, side_rows = planned
        got_rows = flip(side_rows, 2)
    near_keys = lax.ppermute(keys, AXES, near)
    side_values = lax.ppermute(values, AXES, side)
    if plane:
        far_keys = lax.ppermute(side_keys, AXES, compose_route(far, side))
        far_values = lax.ppermute(near_values, AXES, compose_route(far, near))
        relayed = pl.pallas_call(
            relay_kernel,
            out_shape=rows_of(2),
            in_specs=[VMEM] * 3,
            out_specs=VMEM,
            compiler_params=PARAMS,
            cost_estimate=cost(32),
            name="relay_rows",
        )(place, near_rows, got_rows)
        relayed = flip(relayed, 1)
        prefix = [place, own_rows, got_rows, relayed]
    else:
        prefix = [fetch_prefix(seg_len, seg_task, task_slot, prefix_bank, t)]
        far_keys = lax.ppermute(keys, AXES, far)
        far_values = lax.ppermute(values, AXES, far)

    wide = struct((kv_heads, HD, groups * t), jnp.float32)
    flat = struct((kv_heads, groups * t), jnp.float32)
    masks, turned, *state = pl.pallas_call(
        functools.partial(own_kernel, groups, kinds, row_shape[1]),
        out_shape=[
            struct((len(kinds) * t + 2 * row_shape[1], t), jnp.bfloat16),
            struct(wide.shape, queries.dtype),
            wide,
            flat,
            flat,
        ],
        in_specs=[VMEM, HBM, VMEM, VMEM],
        out_specs=[VMEM] * 5,
        scratch_shapes=[pltpu.VMEM(queries.shape, queries.dtype), pltpu.SemaphoreType.DMA],
        compiler_params=PARAMS,
        cost_estimate=cost(8),
        name="attend_own",
    )(place, in_hbm(queries), keys, values)
    state = pl.pallas_call(
        near_kernel,
        out_shape=[wide, flat, flat],
        in_specs=[VMEM] * 9,
        out_specs=[VMEM] * 3,
        compiler_params=PARAMS,
        cost_estimate=cost(2),
        name="attend_near",
    )(masks, turned, near_keys, near_values, side_keys, side_values, *state)
    return pl.pallas_call(
        functools.partial(far_kernel, groups, plane, kinds[-1]),
        out_shape=struct(queries.shape, queries.dtype),
        in_specs=[VMEM] * (7 + len(prefix)),
        out_specs=HBM,
        scratch_shapes=[
            pltpu.VMEM(queries.shape, queries.dtype),
            pltpu.SemaphoreType.DMA((kv_heads,)),
        ],
        compiler_params=PARAMS,
        cost_estimate=cost(4),
        name="attend_far",
    )(masks, turned, far_keys, far_values, *prefix, *state)


def fetch_prefix(seg_len, seg_task, task_slot, prefix_bank, t):
    grp_count = lax.axis_size("grp")
    me = lax.axis_index("grp")
    held = prefix_bank.shape[1]
    starts = jnp.cumsum(seg_len[0]) - seg_len[0]
    shards = lax.axis_index("ctx") * grp_count + jnp.arange(grp_count, dtype=jnp.int32)
    ends = shards[:, None] * t + jnp.array([0, t - 1], jnp.int32)
    segs = jnp.sum((starts[None, None, :] <= ends[:, :, None]).astype(jnp.int32), axis=2) - 1
    rows = task_slot[seg_task[0][segs]]
    local = jnp.clip(rows - me * held, 0, held - 1)
    pieces = jnp.swapaxes(prefix_bank, 0, 1)[local]
    got = lax.all_to_all(pieces, "grp", split_axis=0, concat_axis=0, tiled=True)
    owner = rows[me] // held
    return jnp.stack([got[owner[s], s] for s in range(2)])


def solution(mesh):
    in_specs = (
        P(None, AXES, None),
        P(None, None, AXES, None),
        P(),
        P(),
        P(),
        P(None, "grp", None, None),
    )
    return jax.shard_map(
        on_device, mesh=mesh, in_specs=in_specs, out_specs=P(None, AXES, None), check_vma=False
    )
```
